128 devices in a mesh: batch: 16 (over z, y), seq: 8 (over x, core).
Axes of the slice: x: 4, y: 4, z: 4, core: 2. Of those that a mesh axis runs over, the one named last changes fastest.
Arguments:
- tokens: bfloat16 [32, 1024, 1024], P('batch', 'seq'), may hold values from -6 to 6
- w_in: bfloat16 [1024, 3, 1024], P('batch', None, 'seq'), may hold values from -0.1875 to 0.1875
- w_out: bfloat16 [1024, 1024], P('seq', 'batch'), may hold values from -0.1875 to 0.1875
- conv_weight: bfloat16 [3, 1024], replicated, may hold values from -3.5 to 3.5
- gain_norm: bfloat16 [1024], replicated, may hold values from 0.5 to 1.5
- gain_ffn: bfloat16 [1024], replicated, may hold values from 0.5 to 1.5
- w_gate: bfloat16 [1024, 4608], P('batch', 'seq'), may hold values from -0.1875 to 0.1875
- w_up: bfloat16 [1024, 4608], P('batch', 'seq'), may hold values from -0.1875 to 0.1875
- w_down: bfloat16 [4608, 1024], P('seq', 'batch'), may hold values from -0.09375 to 0.09375
- cotangent: bfloat16 [32, 1024, 1024], P('batch', 'seq'), may hold values from -6 to 6
Outputs:
- output: bfloat16 [32, 1024, 1024], P('batch', 'seq')
- grad_tokens: bfloat16 [32, 1024, 1024], P('batch', 'seq')
- grad_w_in: float32 [1024, 3, 1024], P('batch', None, 'seq')
- grad_w_out: float32 [1024, 1024], P('seq', 'batch')
- grad_conv: float32 [3, 1024], replicated
- grad_gain_norm: float32 [1024], replicated
- grad_gain_ffn: float32 [1024], replicated
- grad_w_gate: float32 [1024, 4608], P('batch', 'seq')
- grad_w_up: float32 [1024, 4608], P('batch', 'seq')
- grad_w_down: float32 [4608, 1024], P('seq', 'batch')
The draws below stay inside these ranges and needn't reach their ends.
All inputs are finite; a program needn't handle non-finite values.
Results may differ from the reference program's by a relative error of at most 0.02.
Values may be sent and summed in bfloat16 or wider, within the bound.
No kernel may reach another device: no remote copies, remote signals or barrier semaphores. Data moves between devices by JAX's collectives and lax.ppermute only.
A program may use at most 192 MiB of HBM per device.

```python
import jax
import jax.numpy as jnp
from jax import lax

D = 1024
FF = 4608
LENGTH = 1024
SEQS = 32


def block_scale(own_key, extent, split, least, high):
    def one(dim, shards_of):
        heights = jax.random.uniform(jax.random.fold_in(jax.random.fold_in(own_key, 6), dim), (shards_of,), jnp.float32, least / len(split), high / len(split))
        return jnp.repeat(jnp.exp(heights), extent[dim] // shards_of).reshape((-1,) + (1,) * (len(extent) - dim - 1))

    factor_of = one(*split[0])
    for cut in split[1:]:
        factor_of = factor_of * one(*cut)
    return factor_of


def centred(stream_key, shape, deviation, reach, pieces=(), dtype=jnp.bfloat16):
    values = deviation * jax.random.normal(stream_key, shape, jnp.float32)
    if pieces:
        values = values * block_scale(stream_key, shape, pieces, -0.22, 0.18)
    return jnp.clip(values, -reach, reach).astype(dtype)


def setup_inputs(seed: int = 0) -> dict:
    seeds = jax.random.split(jax.random.key(seed), 11)
    tokens = centred(seeds[0], (SEQS, LENGTH, D), 1.0, 6.0, ((0, 16), (1, 8)))
    w_in = centred(seeds[1], (D, 3, D), D ** -0.5, 0.1875, ((0, 16), (2, 8)))
    w_out = centred(seeds[2], (D, D), D ** -0.5, 0.1875, ((0, 8), (1, 16)))
    conv_weight = centred(seeds[3], (3, D), 3 ** -0.5, 3.5)
    gain_norm = jnp.clip(1.0 + 0.1 * jax.random.normal(seeds[4], (D,), jnp.float32), 0.5, 1.5).astype(jnp.bfloat16)
    gain_ffn = jnp.clip(1.0 + 0.1 * jax.random.normal(seeds[5], (D,), jnp.float32), 0.5, 1.5).astype(jnp.bfloat16)
    w_gate = centred(seeds[6], (D, FF), D ** -0.5, 0.1875, ((0, 16), (1, 8)))
    w_up = centred(seeds[7], (D, FF), D ** -0.5, 0.1875, ((0, 16), (1, 8)))
    w_down = centred(seeds[8], (FF, D), FF ** -0.5, 0.09375, ((0, 8), (1, 16)))
    cotangent = centred(seeds[9], (SEQS, LENGTH, D), 1.0, 6.0, ((0, 16), (1, 8)))
    return dict(tokens=tokens, w_in=w_in, w_out=w_out, conv_weight=conv_weight, gain_norm=gain_norm, gain_ffn=gain_ffn, w_gate=w_gate, w_up=w_up, w_down=w_down, cotangent=cotangent)


eps = 1e-05

@jax.custom_vjp
def low(v):
    return lax.optimization_barrier(v.astype(jnp.bfloat16)).astype(jnp.float32)

@jax.custom_vjp
def low_back(v):
    return v

def low_keep(v):
    return (low(v), None)

def low_pass(kept, grad):
    return (grad,)

def back_keep(v):
    return (v, None)

def back_low(kept, grad):
    return (low(grad),)
low.defvjp(low_keep, low_pass)
low_back.defvjp(back_keep, back_low)

def rmsnorm(value, gain):
    return value * lax.rsqrt(lax.optimization_barrier(jnp.mean(value * value, -1, keepdims=True)) + eps) * gain

def matmul(left, right):
    return jnp.einsum('nld,de->nle', left, right, precision=lax.Precision.HIGHEST)

def forward(tokens, w_in, w_out, conv_weight, gain_norm, gain_ffn, w_gate, w_up, w_down):
    width = tokens.shape[-1]
    span = tokens.shape[1]
    normed = low(rmsnorm(tokens, gain_norm))
    proj = low_back(matmul(normed, w_in.reshape(width, 3 * width)))
    b_part = proj[..., :width]
    c_part = proj[..., width:2 * width]
    x_part = proj[..., 2 * width:]
    bx_value = low_back(low(b_part * x_part))
    padded = jnp.pad(bx_value, ((0, 0), (2, 0), (0, 0)))
    conv = conv_weight[0] * padded[:, :span] + conv_weight[1] * padded[:, 1:span + 1] + conv_weight[2] * padded[:, 2:]
    gated = low(c_part * conv)
    resid = tokens + low_back(matmul(gated, w_out))
    normed_ffn = low(rmsnorm(resid, gain_ffn))
    gate = low_back(matmul(normed_ffn, w_gate))
    up_value = low_back(matmul(normed_ffn, w_up))
    hidden = low(jax.nn.silu(gate) * up_value)
    return resid + low_back(matmul(hidden, w_down))

def reference(tokens, w_in, w_out, conv_weight, gain_norm, gain_ffn, w_gate, w_up, w_down, cotangent):
    group = 4 if SEQS % 4 == 0 else 1
    blocks = SEQS // group
    weights = tuple((w.astype(jnp.float32) for w in (w_in, w_out, conv_weight, gain_norm, gain_ffn, w_gate, w_up, w_down)))
    inputs = tokens.astype(jnp.float32).reshape(blocks, group, LENGTH, D)
    grads_in = cotangent.astype(jnp.float32).reshape(blocks, group, LENGTH, D)

    def step(totals, item):
        block_in, block_ct = item
        result, pull = jax.vjp(forward, block_in, *weights)
        grads = pull(block_ct)
        totals = tuple((a + g for a, g in zip(totals, grads[1:])))
        return (totals, (result.astype(jnp.bfloat16), grads[0].astype(jnp.bfloat16)))
    start = tuple((jnp.zeros(w.shape, jnp.float32) for w in weights))
    totals, (results, grad_inputs) = lax.scan(step, start, (inputs, grads_in))
    return (results.reshape(SEQS, LENGTH, D), grad_inputs.reshape(SEQS, LENGTH, D), totals[0], totals[1], totals[2], totals[3], totals[4], totals[5], totals[6], totals[7])
```

```python
import jax
import jax.numpy as jnp
from jax import lax
from jax.experimental import pallas as pl
from jax.experimental.pallas import tpu as pltpu
from jax.sharding import PartitionSpec as P

eps = 1e-05
f32 = jnp.float32
bf16 = jnp.bfloat16
width = 1024
rows = 256
part = 128
hid = 576
MIB = 1 << 20


def swap_core(v):
    return lax.ppermute(v, "seq", [(i, i ^ 1) for i in range(8)])


def shift_x(v, d):
    return lax.ppermute(
        v, "seq", [(2 * x + c, 2 * ((x + d) % 4) + c) for x in range(4) for c in range(2)]
    )


def shift_y(v, d):
    return lax.ppermute(
        v, "batch", [(4 * z + y, 4 * z + (y + d) % 4) for z in range(4) for y in range(4)]
    )


def shift_z(v, d):
    return lax.ppermute(
        v, "batch", [(4 * z + y, 4 * ((z + d) % 4) + y) for z in range(4) for y in range(4)]
    )


def sum_over(shifts, v):
    for shift in shifts:
        v = v + shift(v, 1) + shift(v, 2) + shift(v, 3)
    return v


def after(values, *others):
    return lax.optimization_barrier((values, others))[0]


def dot(left, right, dims):
    return lax.dot_general(left, right, (dims, ((), ())), preferred_element_type=f32)


nn = ((1,), (0,))
nt = ((1,), (1,))
tn = ((0,), (0,))


def call(kernel, outs, *args, scratch=(), limit=56, smem=0, name=None):
    specs = [pl.BlockSpec(memory_space=pltpu.SMEM)] * smem + [
        pl.BlockSpec(memory_space=pltpu.VMEM)
    ] * (len(args) - smem)
    shapes = [jax.ShapeDtypeStruct(s, t) for s, t in outs]
    moved = sum(a.size * a.dtype.itemsize for a in args) + sum(
        s.size * s.dtype.itemsize for s in shapes
    )
    return pl.pallas_call(
        kernel,
        out_shape=shapes,
        in_specs=specs,
        out_specs=[pl.BlockSpec(memory_space=pltpu.VMEM)] * len(outs),
        scratch_shapes=list(scratch),
        compiler_params=pltpu.CompilerParams(vmem_limit_bytes=limit * MIB),
        cost_estimate=pl.CostEstimate(flops=1, bytes_accessed=1, transcendentals=0),
        name=name,
    )(*args)


ORDER = [(d, o) for d in (0, 1, 3, 2) for o in (0, 1)]


def k_norm(x_ref, gain_ref, out_ref):
    x = x_ref[...].astype(f32)
    scale = lax.rsqrt(jnp.mean(x * x, -1, keepdims=True) + eps)
    out_ref[...] = (x * scale * gain_ref[...].astype(f32)).astype(bf16)


def k_conv(where_ref, *refs):
    blocks = refs[:8]
    cw_ref, taps_ref, gated_ref, proj_ref, seq_ref = refs[8:]
    win = cw_ref[:, :, : 3 * part].reshape(width, 3 * part)
    seq_ref[:, :8, :] = jnp.zeros((2, 8, part), f32)
    for j in range(8):
        place = where_ref[j]
        proj = dot(blocks[j][...], win, nn)
        proj_ref[place] = proj
        bx = (proj[:, :part] * proj[:, 2 * part :]).astype(bf16).astype(f32)
        start = pl.multiple_of(8 + 128 * place, 8)
        seq_ref[:, pl.ds(start, 128), :] = bx.reshape(2, 128, part)
    taps = taps_ref[...].astype(f32)
    for i in range(8):
        for s in range(2):
            lo = 128 * i
            conv = (
                taps[0:1] * seq_ref[s, lo + 6 : lo + 134, :]
                + taps[1:2] * seq_ref[s, lo + 7 : lo + 135, :]
                + taps[2:3] * seq_ref[s, lo + 8 : lo + 136, :]
            )
            here = slice(128 * s, 128 * s + 128)
            gated_ref[i, here, :] = (proj_ref[i, here, part : 2 * part] * conv).astype(bf16)


def k_resid(where_ref, gated_ref, mine_ref, other_ref, x_ref, gain_ref, resid_ref, out_ref):
    total = x_ref[...].astype(f32)
    for j, (d, o) in enumerate(ORDER):
        weight = (mine_ref, other_ref)[o][j // 2]
        total = total + dot(gated_ref[where_ref[j]], weight, nt)
    resid_ref[...] = total
    scale = lax.rsqrt(jnp.mean(total * total, -1, keepdims=True) + eps)
    out_ref[...] = (total * scale * gain_ref[...].astype(f32)).astype(bf16)


def k_ffn(where_ref, nm, no, ym, yo, w_ref, pm, po, om, oo, h_ref, g_ref):
    wg = w_ref[:, 0].reshape(width, hid)
    wu = w_ref[:, 1].reshape(width, hid)
    wd = w_ref[:, 2].reshape(width, hid)
    for o, (n, y, p, q) in enumerate(((nm, ym, pm, om), (no, yo, po, oo))):
        here = slice(rows * o, rows * o + rows)
        gate = dot(n[...], wg, nn)
        up = dot(n[...], wu, nn)
        back = dot(y[0], wd, nn)
        sigma = jax.nn.sigmoid(gate)
        silu = gate * sigma
        h = (silu * up).astype(bf16)
        gg = (back * up * sigma * (1.0 + gate * (1.0 - sigma))).astype(bf16)
        gu = (back * silu).astype(bf16)
        h_ref[here] = h
        g_ref[0, here] = gg
        g_ref[1, here] = gu
        p[...] = (dot(gg, wg, nt) + dot(gu, wu, nt)).astype(bf16)
        q[...] = dot(h, wd, nt).astype(bf16)


def ffn(where, mine, other, dy_all, weights):
    block = pl.BlockSpec((rows, width), lambda t, w: (0, 0))
    return pl.pallas_call(
        k_ffn,
        out_shape=[jax.ShapeDtypeStruct((rows, width), bf16)] * 4
        + [
            jax.ShapeDtypeStruct((2 * rows, hid), bf16),
            jax.ShapeDtypeStruct((2, 2 * rows, hid), bf16),
        ],
        grid_spec=pltpu.PrefetchScalarGridSpec(
            num_scalar_prefetch=1,
            grid=(1,),
            in_specs=[
                block,
                block,
                pl.BlockSpec((1, rows, width), lambda t, w: (w[0], 0, 0)),
                pl.BlockSpec((1, rows, width), lambda t, w: (w[1], 0, 0)),
                pl.BlockSpec((16, 3, 64, hid), lambda t, w: (0, 0, 0, 0)),
            ],
            out_specs=[block] * 4
            + [
                pl.BlockSpec((2 * rows, hid), lambda t, w: (0, 0)),
                pl.BlockSpec((2, 2 * rows, hid), lambda t, w: (0, 0, 0)),
            ],
        ),
        compiler_params=pltpu.CompilerParams(vmem_limit_bytes=56 * MIB),
        cost_estimate=pl.CostEstimate(flops=1, bytes_accessed=1, transcendentals=0),
        name="ffn",
    )(where, mine, other, dy_all, dy_all, weights)


def k_ffn_grad(where_ref, *refs):
    ns, y_ref = refs[:8], refs[8]
    hs, gs = refs[9:13], refs[13:17]
    out_ref = refs[17]
    tile = ns[0].shape[1]
    for k in range(3):
        total = jnp.zeros((tile, hid), f32)
        for j in range(8):
            here = slice(rows * (j % 2), rows * (j % 2) + rows)
            if k < 2:
                total += dot(ns[j][...], gs[j // 2][k, here], tn)
            else:
                total += dot(y_ref[where_ref[j]], hs[j // 2][here], tn)
        out_ref[:, k] = total.astype(bf16).reshape(tile // 64, 64, hid)


def ffn_grad(where, ns, dy_all, hs, gs):
    tile = 256
    col = pl.BlockSpec((rows, tile), lambda t: (0, t))
    h_spec = pl.BlockSpec((2 * rows, hid), lambda t: (0, 0))
    g_spec = pl.BlockSpec((2, 2 * rows, hid), lambda t: (0, 0, 0))
    return pl.pallas_call(
        k_ffn_grad,
        grid=(width // tile,),
        out_shape=jax.ShapeDtypeStruct((16, 3, 64, hid), bf16),
        in_specs=[pl.BlockSpec(memory_space=pltpu.SMEM)]
        + [col] * 8
        + [pl.BlockSpec((8, rows, tile), lambda t: (0, 0, t))]
        + [h_spec] * 4
        + [g_spec] * 4,
        out_specs=pl.BlockSpec((tile // 64, 3, 64, hid), lambda t: (t, 0, 0, 0)),
        compiler_params=pltpu.CompilerParams(vmem_limit_bytes=56 * MIB),
        cost_estimate=pl.CostEstimate(flops=1, bytes_accessed=1, transcendentals=0),
        name="ffn_grad",
    )(where, *ns, dy_all, *hs, *gs)


def k_mid(where_ref, pm, sw, r1, r3, r2, resid_ref, y_ref, gain_ref, mine_ref, other_ref,
          gres_ref, low_ref, gg_ref, ggain_ref):
    total = pm[...].astype(f32) + sw[...].astype(f32)
    for r in (r1, r3, r2):
        total = total + r[...].astype(f32)
    resid = resid_ref[...]
    scale = lax.rsqrt(jnp.mean(resid * resid, -1, keepdims=True) + eps)
    unit = resid * scale
    ggain_ref[...] = jnp.sum(total * unit, 0, keepdims=True)
    scaled = total * gain_ref[...].astype(f32)
    inner = jnp.mean(scaled * resid, -1, keepdims=True)
    grad = y_ref[...].astype(f32) + scale * (scaled - unit * scale * inner)
    gres_ref[...] = grad
    low = grad.astype(bf16)
    low_ref[...] = low
    for j, (d, o) in enumerate(ORDER):
        weight = (mine_ref, other_ref)[o][j // 2]
        gg_ref[where_ref[j]] = dot(low, weight, nn).astype(bf16)


def k_wout(where_ref, low_ref, gated_ref, keep_ref, send_ref):
    low = low_ref[...]
    for j, (d, o) in enumerate(ORDER):
        out = (keep_ref, send_ref)[o]
        out[j // 2] = dot(low, gated_ref[where_ref[j]], tn).astype(bf16)


def k_conv_back(where_ref, dg_ref, proj_ref, cw_ref, taps_ref, *refs):
    outs = refs[:8]
    dp_ref, gtaps_ref, seq_ref, back_ref, abs_ref = refs[8:]
    win = cw_ref[:, :, : 3 * part].reshape(width, 3 * part)
    taps = taps_ref[...].astype(f32)
    seq_ref[:, :8, :] = jnp.zeros((2, 8, part), f32)
    back_ref[:, 1024:, :] = jnp.zeros((2, 8, part), f32)
    for i in range(8):
        for s in range(2):
            here = slice(128 * s, 128 * s + 128)
            lo = 128 * i
            b = proj_ref[i, here, :part]
            x = proj_ref[i, here, 2 * part :]
            seq_ref[s, lo + 8 : lo + 136, :] = (b * x).astype(bf16).astype(f32)
            c = proj_ref[i, here, part : 2 * part]
            back_ref[s, lo : lo + 128, :] = dg_ref[i, here, :].astype(f32) * c
    sums = [jnp.zeros((1, part), f32) for _ in range(3)]
    for i in range(8):
        for s in range(2):
            here = slice(128 * s, 128 * s + 128)
            lo = 128 * i
            back = back_ref[s, lo : lo + 128, :]
            shifted = [seq_ref[s, lo + 6 + k : lo + 134 + k, :] for k in range(3)]
            conv = taps[0:1] * shifted[0] + taps[1:2] * shifted[1] + taps[2:3] * shifted[2]
            for k in range(3):
                sums[k] = sums[k] + jnp.sum(back * shifted[k], 0, keepdims=True)
            dbx = (
                taps[0:1] * back_ref[s, lo + 2 : lo + 130, :]
                + taps[1:2] * back_ref[s, lo + 1 : lo + 129, :]
                + taps[2:3] * back
            )
            dbx = dbx.astype(bf16).astype(f32)
            abs_ref[i, here, :part] = (dbx * proj_ref[i, here, 2 * part :]).astype(bf16)
            abs_ref[i, here, part : 2 * part] = (
                dg_ref[i, here, :].astype(f32) * conv
            ).astype(bf16)
            abs_ref[i, here, 2 * part :] = (dbx * proj_ref[i, here, :part]).astype(bf16)
    gtaps_ref[...] = jnp.concatenate(sums + [jnp.zeros((5, part), f32)], 0)
    for j in range(8):
        piece = abs_ref[where_ref[j]]
        dp_ref[j] = piece
        outs[j][...] = dot(piece, win, nt).astype(bf16)


def k_win(where_ref, *refs):
    blocks = refs[:8]
    dp_ref, cw_ref, gtaps_ref, gain_ref, ggain_ref, out_ref, small_ref = refs[8:]
    total = jnp.zeros((width, 3 * part), f32)
    for j in range(8):
        total += dot(blocks[j][...], dp_ref[j], tn)
    out_ref[...] = total.astype(bf16)
    win = cw_ref[:, :, : 3 * part].reshape(width, 3 * part)
    each = jnp.sum(total * win.astype(f32), 1, keepdims=True)
    line = jnp.transpose(jnp.broadcast_to(each, (width, part)))[:1]
    small_ref[...] = jnp.concatenate(
        [
            jnp.zeros((3, width), f32),
            line / gain_ref[...].astype(f32),
            ggain_ref[...],
            jnp.zeros((3, width), f32),
        ],
        0,
    )
    here = pl.ds(pl.multiple_of(where_ref[0] * part, part), part)
    small_ref[:3, here] = gtaps_ref[:3]


def k_fin(pm, sw, r1, r3, r2, x_ref, gres_ref, gain_ref, out_ref):
    total = pm[...].astype(f32) + sw[...].astype(f32)
    for r in (r1, r3, r2):
        total = total + r[...].astype(f32)
    x = x_ref[...].astype(f32)
    scale = lax.rsqrt(jnp.mean(x * x, -1, keepdims=True) + eps)
    scaled = total * gain_ref[...].astype(f32)
    inner = jnp.mean(scaled * x, -1, keepdims=True)
    out_ref[...] = (
        gres_ref[...] + scale * (scaled - x * scale * scale * inner)
    ).astype(bf16)


def pair_sum(mine, other):
    return (mine.astype(f32) + other.astype(f32)).astype(bf16)


def shards(tokens, w_in, w_out, conv_weight, gain_norm, gain_ffn, w_gate, w_up, w_down, cotangent):
    place = lax.axis_index("seq")
    core = place % 2
    chip = place // 2
    where = jnp.stack(
        [2 * ((chip - d + 4) % 4) + (core if o == 0 else 1 - core) for d, o in ORDER]
    ).astype(jnp.int32)
    taps = lax.dynamic_slice(conv_weight, (0, place * part), (3, part))
    gain_one = gain_norm.reshape(1, width)
    gain_two = gain_ffn.reshape(1, width)
    x = tokens.reshape(rows, width)
    dy = cotangent.reshape(rows, width)

    ffn_local = jnp.stack([w_gate, w_up, w_down.T], 0)
    ffn_w = lax.all_gather(ffn_local, "batch", axis=0, tiled=False)
    (normed,) = call(k_norm, [((rows, width), bf16)], x, gain_one, name="norm")
    with jax.named_scope("normed"):
        got = {d: shift_x(normed, d) for d in (1, 3, 2)}
        got[0] = normed
        swapped = {d: swap_core(got[d]) for d in (0, 1, 3, 2)}
        normed_list = [(got, swapped)[o][d] for d, o in ORDER]
    with jax.named_scope("conv_weights"):
        conv_local = jnp.concatenate([w_in.reshape(64, 3 * part), w_out.T], 1)
        conv_w = lax.all_to_all(jnp.broadcast_to(conv_local[None], (16, 64, 512)), "batch", 0, 0)

    gated, proj = call(
        k_conv, [((8, rows, part), bf16), ((8, rows, 3 * part), f32)],
        where, *normed_list, conv_w, taps, smem=1,
        scratch=[pltpu.VMEM((2, 1032, part), f32)], name="conv",
    )
    with jax.named_scope("gated"):
        gated_tok = lax.all_to_all(gated, "seq", 0, 0)
    with jax.named_scope("w_out"):
        wout_own = after(conv_w[:, :, 3 * part :].reshape(width, part), proj)
        wout_got = tuple(shift_x(wout_own, d) for d in (1, 3, 2))
        gated_tok, wout_got = lax.optimization_barrier((gated_tok, wout_got))
        wout_mine = jnp.stack((wout_own,) + wout_got, 0)
        wout_other = swap_core(wout_mine)
    dy_all = lax.all_gather(after(dy, ffn_w, gated_tok), "seq", axis=0, tiled=False)
    resid, nffn = call(
        k_resid, [((rows, width), f32), ((rows, width), bf16)],
        where, gated_tok, wout_mine, wout_other, x, gain_two, smem=1, name="resid",
    )

    with jax.named_scope("normed_ffn"):
        nffn_got = {d: shift_x(nffn, d) for d in (1, 3, 2)}
        nffn_got[0] = nffn
        nffn_swapped = {0: swap_core(nffn)}
    blocks, back_swap, out_swap, back_low, out_low = {}, {}, {}, {}, {}
    blocks[0] = ffn(where[:2], nffn, nffn_swapped[0], dy_all, ffn_w)
    with jax.named_scope("normed_ffn"):
        arrived, blocks[0] = lax.optimization_barrier(
            (tuple(nffn_got[d] for d in (1, 3, 2)), tuple(blocks[0]))
        )
        for d, piece in zip((1, 3, 2), arrived):
            nffn_got[d] = piece
            nffn_swapped[d] = swap_core(piece)
    nffn_list = [(nffn_got, nffn_swapped)[o][d] for d, o in ORDER]
    for n, d in enumerate((0, 1, 3, 2)):
        if d:
            blocks[d] = ffn(
                where[2 * n : 2 * n + 2], nffn_got[d], nffn_swapped[d], dy_all, ffn_w
            )
        with jax.named_scope("grad_normed_ffn"):
            back_swap[d] = swap_core(blocks[d][1])
            if d:
                back_low[d] = pair_sum(blocks[d][0], back_swap[d])
    grad_in = (
        where, nffn_list, dy_all, [blocks[d][4] for d in (0, 1, 3, 2)],
        [blocks[d][5] for d in (0, 1, 3, 2)],
    )
    with jax.named_scope("grad_normed_ffn"):
        grad_in, back_low = lax.optimization_barrier((grad_in, back_low))
        back_got = {d: shift_x(back_low[d], (4 - d) % 4) for d in (1, 3, 2)}
    ffn_g = ffn_grad(*grad_in)
    gres, low, dgated, ggain_two = call(
        k_mid,
        [((rows, width), f32), ((rows, width), bf16), ((8, rows, part), bf16), ((1, width), f32)],
        where, after(blocks[0][0], ffn_g), back_swap[0], back_got[1],
        back_got[3], back_got[2], resid, dy, gain_two, wout_mine, wout_other, smem=1,
        name="mid",
    )
    with jax.named_scope("ffn_grads"):
        ffn_sent = lax.psum_scatter(after(ffn_g, low), "batch", scatter_dimension=0, tiled=False)
    with jax.named_scope("grad_gated"):
        dgated_all = lax.all_to_all(dgated, "seq", 0, 0)

    wout_keep, wout_send = call(
        k_wout, [((4, width, part), bf16)] * 2, where, low, gated_tok, smem=1, name="wout",
    )
    with jax.named_scope("grad_w_out"):
        wout_both = wout_keep.astype(f32) + swap_core(wout_send).astype(f32)
        wout_low = wout_both.astype(bf16)
    with jax.named_scope("output"):
        out_parts = {d: after((blocks[d][2], blocks[d][3]), low) for d in (1, 0, 3, 2)}
        for d in (1, 3, 2, 0):
            out_swap[d] = swap_core(out_parts[d][1])
        for d in (1, 3, 2):
            out_low[d] = pair_sum(out_parts[d][0], out_swap[d])
        out_got = {d: shift_x(out_low[d], (4 - d) % 4) for d in (1, 3)}
    with jax.named_scope("grad_w_out"):
        grad_wout = wout_both[0]
        wout_back = [shift_x(wout_low[j], (4 - d) % 4) for j, d in ((1, 1), (2, 3), (3, 2))]
    dgated_all, out_got, wout_back, out_low = lax.optimization_barrier(
        (dgated_all, out_got, wout_back, out_low)
    )
    with jax.named_scope("grad_w_out"):
        for piece in wout_back:
            grad_wout = grad_wout + piece.astype(f32)

    conv_back = call(
        k_conv_back,
        [((rows, width), bf16)] * 8 + [((8, rows, 3 * part), bf16), ((8, part), f32)],
        where, dgated_all, proj, conv_w, taps, smem=1,
        scratch=[
            pltpu.VMEM((2, 1032, part), f32),
            pltpu.VMEM((2, 1032, part), f32),
            pltpu.VMEM((8, rows, 3 * part), bf16),
        ],
        name="conv_back",
    )
    part_of = {(d, o): conv_back[j] for j, (d, o) in enumerate(ORDER)}
    dproj, gtaps = conv_back[8:]
    with jax.named_scope("grad_normed"):
        dn_swap = {d: swap_core(part_of[(d, 1)]) for d in (1, 3, 2, 0)}
    grad_win, small = call(
        k_win, [((width, 3 * part), bf16), ((8, width), f32)],
        where, *normed_list, dproj, conv_w, gtaps, gain_one, ggain_two, smem=1, name="win",
    )
    with jax.named_scope("grad_normed"):
        dn_keep = {d: part_of[(d, 0)] for d in (1, 3, 2)}
        dn_keep = after(dn_keep, grad_win)
        dn_low = {d: pair_sum(dn_keep[d], dn_swap[d]) for d in (1, 3, 2)}
        dn_got = {d: shift_x(dn_low[d], (4 - d) % 4) for d in (1, 3)}
    with jax.named_scope("vectors"):
        small = after(small, *dn_low.values())
        small = sum_over((shift_z,), small)
    grad_cw = jnp.concatenate([grad_win, grad_wout.astype(bf16)], 1)
    last_in = (dn_low[2], out_low[2], grad_cw, small)
    last_in, sum_ffn = after((last_in, ffn_sent.astype(f32)), dn_got[1], dn_got[3])
    with jax.named_scope("conv_grads"):
        cw_sent = lax.all_to_all(last_in[2].reshape(16, 64, 512), "batch", 0, 0)
    with jax.named_scope("grad_normed"):
        dn_got[2] = shift_x(last_in[0], 2)
    with jax.named_scope("output"):
        out_got[2] = shift_x(last_in[1], 2)
    with jax.named_scope("vectors"):
        small = sum_over((shift_y,), last_in[3])
    cw_sent, dn_got, out_got, small = lax.optimization_barrier(
        (cw_sent, dn_got, out_got, small)
    )
    with jax.named_scope("vectors"):
        small = sum_over((shift_x,), small)
        small = small + swap_core(small)
    with jax.named_scope("conv_grads"):
        sum_cw = jnp.sum(cw_sent.astype(f32), 0)
    result = resid + out_parts[0][0].astype(f32) + out_swap[0].astype(f32)
    for d in (1, 3, 2):
        result = result + out_got[d].astype(f32)
    output = result.astype(bf16).reshape(2, 128, width)
    (grad_tokens,) = call(
        k_fin, [((rows, width), bf16)],
        part_of[(0, 0)], dn_swap[0], dn_got[1], dn_got[3], dn_got[2], x, gres, gain_one,
        name="fin",
    )
    return (
        output,
        grad_tokens.reshape(2, 128, width),
        sum_cw[:, : 3 * part].reshape(64, 3, part),
        sum_cw[:, 3 * part :].T,
        small[:3],
        small[3],
        small[4],
        sum_ffn[0],
        sum_ffn[1],
        sum_ffn[2].T,
    )


def solution(mesh):
    whole = P("batch", "seq", None)
    placed = (
        whole, P("batch", None, "seq"), P("seq", "batch"), P(), P(), P(),
        P("batch", "seq"), P("batch", "seq"), P("seq", "batch"), whole,
    )
    return jax.shard_map(
        shards,
        mesh=mesh,
        in_specs=placed,
        out_specs=(
            whole, whole, P("batch", None, "seq"), P("seq", "batch"), P(), P(), P(),
            P("batch", "seq"), P("batch", "seq"), P("seq", "batch"),
        ),
        check_vma=False,
    )
```

```python
import jax
import jax.numpy as jnp
from jax import lax
from jax.experimental import pallas as pl
from jax.experimental.pallas import tpu as pltpu
from jax.sharding import PartitionSpec as P

eps = 1e-05
f32 = jnp.float32
bf16 = jnp.bfloat16
width = 1024
rows = 256
part = 128
hid = 576
MIB = 1 << 20


def swap_core(v):
    return lax.ppermute(v, "seq", [(i, i ^ 1) for i in range(8)])


def shift_x(v, d):
    return lax.ppermute(
        v, "seq", [(2 * x + c, 2 * ((x + d) % 4) + c) for x in range(4) for c in range(2)]
    )


def shift_y(v, d):
    return lax.ppermute(
        v, "batch", [(4 * z + y, 4 * z + (y + d) % 4) for z in range(4) for y in range(4)]
    )


def shift_z(v, d):
    return lax.ppermute(
        v, "batch", [(4 * z + y, 4 * ((z + d) % 4) + y) for z in range(4) for y in range(4)]
    )


def sum_over(shifts, v):
    for shift in shifts:
        v = v + shift(v, 1) + shift(v, 2) + shift(v, 3)
    return v


def after(values, *others):
    return lax.optimization_barrier((values, others))[0]


def dot(left, right, dims):
    return lax.dot_general(left, right, (dims, ((), ())), preferred_element_type=f32)


nn = ((1,), (0,))
nt = ((1,), (1,))
tn = ((0,), (0,))


def call(kernel, outs, *args, scratch=(), limit=56, smem=0, name=None):
    specs = [pl.BlockSpec(memory_space=pltpu.SMEM)] * smem + [
        pl.BlockSpec(memory_space=pltpu.VMEM)
    ] * (len(args) - smem)
    shapes = [jax.ShapeDtypeStruct(s, t) for s, t in outs]
    moved = sum(a.size * a.dtype.itemsize for a in args) + sum(
        s.size * s.dtype.itemsize for s in shapes
    )
    return pl.pallas_call(
        kernel,
        out_shape=shapes,
        in_specs=specs,
        out_specs=[pl.BlockSpec(memory_space=pltpu.VMEM)] * len(outs),
        scratch_shapes=list(scratch),
        compiler_params=pltpu.CompilerParams(vmem_limit_bytes=limit * MIB),
        cost_estimate=pl.CostEstimate(flops=1, bytes_accessed=1, transcendentals=0),
        name=name,
    )(*args)


ORDER = [(d, o) for d in (0, 1, 3, 2) for o in (0, 1)]


def k_norm(x_ref, gain_ref, out_ref):
    x = x_ref[...].astype(f32)
    scale = lax.rsqrt(jnp.mean(x * x, -1, keepdims=True) + eps)
    out_ref[...] = (x * scale * gain_ref[...].astype(f32)).astype(bf16)


def k_conv(where_ref, *refs):
    blocks = refs[:8]
    cw_ref, taps_ref, gated_ref, proj_ref, seq_ref = refs[8:]
    win = cw_ref[:, :, : 3 * part].reshape(width, 3 * part)
    seq_ref[:, :8, :] = jnp.zeros((2, 8, part), f32)
    for j in range(8):
        place = where_ref[j]
        proj = dot(blocks[j][...], win, nn)
        proj_ref[place] = proj
        bx = (proj[:, :part] * proj[:, 2 * part :]).astype(bf16).astype(f32)
        start = pl.multiple_of(8 + 128 * place, 8)
        seq_ref[:, pl.ds(start, 128), :] = bx.reshape(2, 128, part)
    taps = taps_ref[...].astype(f32)
    for i in range(8):
        for s in range(2):
            lo = 128 * i
            conv = (
                taps[0:1] * seq_ref[s, lo + 6 : lo + 134, :]
                + taps[1:2] * seq_ref[s, lo + 7 : lo + 135, :]
                + taps[2:3] * seq_ref[s, lo + 8 : lo + 136, :]
            )
            here = slice(128 * s, 128 * s + 128)
            gated_ref[i, here, :] = (proj_ref[i, here, part : 2 * part] * conv).astype(bf16)


def k_resid(where_ref, gated_ref, mine_ref, other_ref, x_ref, gain_ref, resid_ref, out_ref):
    total = x_ref[...].astype(f32)
    for j, (d, o) in enumerate(ORDER):
        weight = (mine_ref, other_ref)[o][j // 2]
        total = total + dot(gated_ref[where_ref[j]], weight, nt)
    resid_ref[...] = total
    scale = lax.rsqrt(jnp.mean(total * total, -1, keepdims=True) + eps)
    out_ref[...] = (total * scale * gain_ref[...].astype(f32)).astype(bf16)


def k_ffn(nm, no, ym, yo, w_ref, pm, po, om, oo, h_ref, g_ref):
    wg = w_ref[:, 0].reshape(width, hid)
    wu = w_ref[:, 1].reshape(width, hid)
    wd = w_ref[:, 2].reshape(width, hid)
    for o, (n, y, p, q) in enumerate(((nm, ym, pm, om), (no, yo, po, oo))):
        here = slice(rows * o, rows * o + rows)
        gate = dot(n[...], wg, nn)
        up = dot(n[...], wu, nn)
        back = dot(y[...], wd, nn)
        sigma = jax.nn.sigmoid(gate)
        silu = gate * sigma
        h = (silu * up).astype(bf16)
        gg = (back * up * sigma * (1.0 + gate * (1.0 - sigma))).astype(bf16)
        gu = (back * silu).astype(bf16)
        h_ref[here] = h
        g_ref[0, here] = gg
        g_ref[1, here] = gu
        p[...] = (dot(gg, wg, nt) + dot(gu, wu, nt)).astype(bf16)
        q[...] = dot(h, wd, nt).astype(bf16)


def k_ffn_grad(*refs):
    ns, ys = refs[:8], refs[8:16]
    hs, gs = refs[16:20], refs[20:24]
    out_ref = refs[24]
    tile = ns[0].shape[1]
    for k in range(3):
        total = jnp.zeros((tile, hid), f32)
        for j in range(8):
            here = slice(rows * (j % 2), rows * (j % 2) + rows)
            if k < 2:
                total += dot(ns[j][...], gs[j // 2][k, here], tn)
            else:
                total += dot(ys[j][...], hs[j // 2][here], tn)
        out_ref[:, k] = total.astype(bf16).reshape(tile // 64, 64, hid)


def ffn_grad(ns, ys, hs, gs):
    tile = 256
    col = pl.BlockSpec((rows, tile), lambda t: (0, t))
    h_spec = pl.BlockSpec((2 * rows, hid), lambda t: (0, 0))
    g_spec = pl.BlockSpec((2, 2 * rows, hid), lambda t: (0, 0, 0))
    return pl.pallas_call(
        k_ffn_grad,
        grid=(width // tile,),
        out_shape=jax.ShapeDtypeStruct((16, 3, 64, hid), bf16),
        in_specs=[col] * 16
        + [h_spec] * 4
        + [g_spec] * 4,
        out_specs=pl.BlockSpec((tile // 64, 3, 64, hid), lambda t: (t, 0, 0, 0)),
        compiler_params=pltpu.CompilerParams(vmem_limit_bytes=56 * MIB),
        cost_estimate=pl.CostEstimate(flops=1, bytes_accessed=1, transcendentals=0),
        name="ffn_grad",
    )(*ns, *ys, *hs, *gs)


def k_mid(where_ref, pm, sw, r1, r3, r2, resid_ref, y_ref, gain_ref, mine_ref, other_ref,
          gres_ref, low_ref, gg_ref, ggain_ref):
    total = pm[...].astype(f32) + sw[...].astype(f32)
    for r in (r1, r3, r2):
        total = total + r[...].astype(f32)
    resid = resid_ref[...]
    scale = lax.rsqrt(jnp.mean(resid * resid, -1, keepdims=True) + eps)
    unit = resid * scale
    ggain_ref[...] = jnp.sum(total * unit, 0, keepdims=True)
    scaled = total * gain_ref[...].astype(f32)
    inner = jnp.mean(scaled * resid, -1, keepdims=True)
    grad = y_ref[...].astype(f32) + scale * (scaled - unit * scale * inner)
    gres_ref[...] = grad
    low = grad.astype(bf16)
    low_ref[...] = low
    for j, (d, o) in enumerate(ORDER):
        weight = (mine_ref, other_ref)[o][j // 2]
        gg_ref[where_ref[j]] = dot(low, weight, nn).astype(bf16)


def k_wout(where_ref, low_ref, gated_ref, keep_ref, send_ref):
    low = low_ref[...]
    for j, (d, o) in enumerate(ORDER):
        out = (keep_ref, send_ref)[o]
        out[j // 2] = dot(low, gated_ref[where_ref[j]], tn).astype(bf16)


def k_conv_back(where_ref, dg_ref, proj_ref, cw_ref, taps_ref, *refs):
    outs = refs[:8]
    dp_ref, gtaps_ref, seq_ref, back_ref, abs_ref = refs[8:]
    win = cw_ref[:, :, : 3 * part].reshape(width, 3 * part)
    taps = taps_ref[...].astype(f32)
    seq_ref[:, :8, :] = jnp.zeros((2, 8, part), f32)
    back_ref[:, 1024:, :] = jnp.zeros((2, 8, part), f32)
    for i in range(8):
        for s in range(2):
            here = slice(128 * s, 128 * s + 128)
            lo = 128 * i
            b = proj_ref[i, here, :part]
            x = proj_ref[i, here, 2 * part :]
            seq_ref[s, lo + 8 : lo + 136, :] = (b * x).astype(bf16).astype(f32)
            c = proj_ref[i, here, part : 2 * part]
            back_ref[s, lo : lo + 128, :] = dg_ref[i, here, :].astype(f32) * c
    sums = [jnp.zeros((1, part), f32) for _ in range(3)]
    for i in range(8):
        for s in range(2):
            here = slice(128 * s, 128 * s + 128)
            lo = 128 * i
            back = back_ref[s, lo : lo + 128, :]
            shifted = [seq_ref[s, lo + 6 + k : lo + 134 + k, :] for k in range(3)]
            conv = taps[0:1] * shifted[0] + taps[1:2] * shifted[1] + taps[2:3] * shifted[2]
            for k in range(3):
                sums[k] = sums[k] + jnp.sum(back * shifted[k], 0, keepdims=True)
            dbx = (
                taps[0:1] * back_ref[s, lo + 2 : lo + 130, :]
                + taps[1:2] * back_ref[s, lo + 1 : lo + 129, :]
                + taps[2:3] * back
            )
            dbx = dbx.astype(bf16).astype(f32)
            abs_ref[i, here, :part] = (dbx * proj_ref[i, here, 2 * part :]).astype(bf16)
            abs_ref[i, here, part : 2 * part] = (
                dg_ref[i, here, :].astype(f32) * conv
            ).astype(bf16)
            abs_ref[i, here, 2 * part :] = (dbx * proj_ref[i, here, :part]).astype(bf16)
    gtaps_ref[...] = jnp.concatenate(sums + [jnp.zeros((5, part), f32)], 0)
    for j in range(8):
        piece = abs_ref[where_ref[j]]
        dp_ref[j] = piece
        outs[j][...] = dot(piece, win, nt).astype(bf16)


def k_win(where_ref, *refs):
    blocks = refs[:8]
    dp_ref, cw_ref, gtaps_ref, gain_ref, ggain_ref, out_ref, small_ref = refs[8:]
    total = jnp.zeros((width, 3 * part), f32)
    for j in range(8):
        total += dot(blocks[j][...], dp_ref[j], tn)
    out_ref[...] = total.astype(bf16)
    win = cw_ref[:, :, : 3 * part].reshape(width, 3 * part)
    each = jnp.sum(total * win.astype(f32), 1, keepdims=True)
    line = jnp.transpose(jnp.broadcast_to(each, (width, part)))[:1]
    small_ref[...] = jnp.concatenate(
        [
            jnp.zeros((3, width), f32),
            line / gain_ref[...].astype(f32),
            ggain_ref[...],
            jnp.zeros((3, width), f32),
        ],
        0,
    )
    here = pl.ds(pl.multiple_of(where_ref[0] * part, part), part)
    small_ref[:3, here] = gtaps_ref[:3]


def k_fin(pm, sw, r1, r3, r2, x_ref, gres_ref, gain_ref, out_ref):
    total = pm[...].astype(f32) + sw[...].astype(f32)
    for r in (r1, r3, r2):
        total = total + r[...].astype(f32)
    x = x_ref[...].astype(f32)
    scale = lax.rsqrt(jnp.mean(x * x, -1, keepdims=True) + eps)
    scaled = total * gain_ref[...].astype(f32)
    inner = jnp.mean(scaled * x, -1, keepdims=True)
    out_ref[...] = (
        gres_ref[...] + scale * (scaled - x * scale * scale * inner)
    ).astype(bf16)


def pair_sum(mine, other):
    return (mine.astype(f32) + other.astype(f32)).astype(bf16)


def shards(tokens, w_in, w_out, conv_weight, gain_norm, gain_ffn, w_gate, w_up, w_down, cotangent):
    place = lax.axis_index("seq")
    core = place % 2
    chip = place // 2
    where = jnp.stack(
        [2 * ((chip - d + 4) % 4) + (core if o == 0 else 1 - core) for d, o in ORDER]
    ).astype(jnp.int32)
    taps = lax.dynamic_slice(conv_weight, (0, place * part), (3, part))
    gain_one = gain_norm.reshape(1, width)
    gain_two = gain_ffn.reshape(1, width)
    x = tokens.reshape(rows, width)
    dy = cotangent.reshape(rows, width)

    ffn_local = jnp.stack([w_gate, w_up, w_down.T], 0)
    ffn_w = lax.all_gather(ffn_local, "batch", axis=0, tiled=False)
    (normed,) = call(k_norm, [((rows, width), bf16)], x, gain_one, name="norm")
    with jax.named_scope("normed"):
        got = {d: shift_x(normed, d) for d in (1, 3, 2)}
        got[0] = normed
        swapped = {d: swap_core(got[d]) for d in (0, 1, 3, 2)}
        normed_list = [(got, swapped)[o][d] for d, o in ORDER]
    with jax.named_scope("conv_weights"):
        conv_local = jnp.concatenate([w_in.reshape(64, 3 * part), w_out.T], 1)
        conv_w = lax.all_to_all(jnp.broadcast_to(conv_local[None], (16, 64, 512)), "batch", 0, 0)

    gated, proj = call(
        k_conv, [((8, rows, part), bf16), ((8, rows, 3 * part), f32)],
        where, *normed_list, conv_w, taps, smem=1,
        scratch=[pltpu.VMEM((2, 1032, part), f32)], name="conv",
    )
    with jax.named_scope("cotangent"):
        dy_late = after(dy, got[1], got[3], got[2])
        dy_got = {d: shift_x(dy_late, d) for d in (1, 3)}
        dy_got[0] = dy
        gated, proj, dy_got = lax.optimization_barrier((gated, proj, dy_got))
        dy_far = shift_x(after(dy, dy_got[1], dy_got[3], proj), 2)
    with jax.named_scope("gated"):
        gated_tok = lax.all_to_all(gated, "seq", 0, 0)
    with jax.named_scope("w_out"):
        wout_own = after(conv_w[:, :, 3 * part :].reshape(width, part), proj)
        wout_got = tuple(shift_x(wout_own, d) for d in (1, 3, 2))
        gated_tok, wout_got, dy_got[2] = lax.optimization_barrier((gated_tok, wout_got, dy_far))
        wout_mine = jnp.stack((wout_own,) + wout_got, 0)
        wout_other = swap_core(wout_mine)
    resid, nffn = call(
        k_resid, [((rows, width), f32), ((rows, width), bf16)],
        where, gated_tok, wout_mine, wout_other, x, gain_two, smem=1, name="resid",
    )

    with jax.named_scope("normed_ffn"):
        nffn_got = {d: shift_x(nffn, d) for d in (1, 3, 2)}
        nffn_got[0] = nffn
        nffn_swapped = {0: swap_core(nffn)}
    blocks, back_swap, out_swap, back_low, out_low = {}, {}, {}, {}, {}
    with jax.named_scope("cotangent"):
        dy_swapped = {d: swap_core(dy_got[d]) for d in (0, 1, 3, 2)}
    dy_list = [(dy_got, dy_swapped)[o][d] for d, o in ORDER]

    def ffn(d):
        return call(
            k_ffn,
            [((rows, width), bf16)] * 4 + [((2 * rows, hid), bf16), ((2, 2 * rows, hid), bf16)],
            nffn_got[d], nffn_swapped[d], dy_got[d], dy_swapped[d], ffn_w, name="ffn",
        )

    blocks[0] = ffn(0)
    with jax.named_scope("normed_ffn"):
        arrived, blocks[0] = lax.optimization_barrier(
            (tuple(nffn_got[d] for d in (1, 3, 2)), tuple(blocks[0]))
        )
        for d, piece in zip((1, 3, 2), arrived):
            nffn_got[d] = piece
            nffn_swapped[d] = swap_core(piece)
    nffn_list = [(nffn_got, nffn_swapped)[o][d] for d, o in ORDER]
    for d in (0, 1, 3, 2):
        if d:
            blocks[d] = ffn(d)
        with jax.named_scope("grad_normed_ffn"):
            back_swap[d] = swap_core(blocks[d][1])
            if d:
                back_low[d] = pair_sum(blocks[d][0], back_swap[d])
        with jax.named_scope("output"):
            out_swap[d] = swap_core(blocks[d][3])
            if d:
                out_low[d] = pair_sum(blocks[d][2], out_swap[d])
    grad_in = (
        nffn_list, dy_list, [blocks[d][4] for d in (0, 1, 3, 2)],
        [blocks[d][5] for d in (0, 1, 3, 2)],
    )
    with jax.named_scope("grad_normed_ffn"):
        grad_in = after(grad_in, back_low, out_low)
        back_got = {d: shift_x(back_low[d], (4 - d) % 4) for d in (1, 3, 2)}
    ffn_g = ffn_grad(*grad_in)
    with jax.named_scope("output"):
        out_ready = after(out_low, ffn_g, *back_got.values())
        out_got = {d: shift_x(out_ready[d], (4 - d) % 4) for d in (1, 3)}
    gres, low, dgated, ggain_two = call(
        k_mid,
        [((rows, width), f32), ((rows, width), bf16), ((8, rows, part), bf16), ((1, width), f32)],
        where, after(blocks[0][0], ffn_g), back_swap[0], back_got[1],
        back_got[3], back_got[2], resid, dy, gain_two, wout_mine, wout_other, smem=1,
        name="mid",
    )
    with jax.named_scope("ffn_grads"):
        ffn_sent = lax.psum_scatter(after(ffn_g, low), "batch", scatter_dimension=0, tiled=False)
    wout_keep, wout_send = call(
        k_wout, [((4, width, part), bf16)] * 2, where, low, gated_tok, smem=1, name="wout",
    )
    with jax.named_scope("grad_gated"):
        dgated_all = lax.all_to_all(dgated, "seq", 0, 0)
    with jax.named_scope("grad_w_out"):
        wout_both = wout_keep.astype(f32) + swap_core(wout_send).astype(f32)
        wout_low = wout_both.astype(bf16)
    with jax.named_scope("grad_w_out"):
        grad_wout = wout_both[0]
    dgated_all, out_got, wout_low, out_low = lax.optimization_barrier(
        (dgated_all, out_got, wout_low, out_low)
    )
    with jax.named_scope("output"):
        out_got[2] = shift_x(out_low[2], 2)
    with jax.named_scope("grad_w_out"):
        wout_back = [shift_x(wout_low[j], (4 - d) % 4) for j, d in ((1, 1), (2, 3), (3, 2))]
        for piece in wout_back:
            grad_wout = grad_wout + piece.astype(f32)

    conv_back = call(
        k_conv_back,
        [((rows, width), bf16)] * 8 + [((8, rows, 3 * part), bf16), ((8, part), f32)],
        where, dgated_all, proj, conv_w, taps, smem=1,
        scratch=[
            pltpu.VMEM((2, 1032, part), f32),
            pltpu.VMEM((2, 1032, part), f32),
            pltpu.VMEM((8, rows, 3 * part), bf16),
        ],
        name="conv_back",
    )
    part_of = {(d, o): conv_back[j] for j, (d, o) in enumerate(ORDER)}
    dproj, gtaps = conv_back[8:]
    with jax.named_scope("grad_normed"):
        dn_swap = {d: swap_core(part_of[(d, 1)]) for d in (1, 3, 2, 0)}
    grad_win, small = call(
        k_win, [((width, 3 * part), bf16), ((8, width), f32)],
        where, *normed_list, dproj, conv_w, gtaps, gain_one, ggain_two, smem=1, name="win",
    )
    with jax.named_scope("grad_normed"):
        dn_keep = {d: part_of[(d, 0)] for d in (1, 3, 2)}
        dn_keep, out_got = lax.optimization_barrier((after(dn_keep, grad_win), out_got))
        dn_low = {d: pair_sum(dn_keep[d], dn_swap[d]) for d in (1, 3, 2)}
        dn_got = {d: shift_x(dn_low[d], (4 - d) % 4) for d in (1, 3)}
    with jax.named_scope("vectors"):
        small = after(small, *dn_low.values())
        small = sum_over((shift_z, shift_y), small)
    grad_cw = jnp.concatenate([grad_win, grad_wout.astype(bf16)], 1)
    last_in = (dn_low[2], grad_cw, small)
    last_in = after(last_in, dn_got[1], dn_got[3])
    with jax.named_scope("conv_grads"):
        grad_cw, sum_ffn = lax.optimization_barrier((last_in[1], ffn_sent.astype(f32)))
        cw_sent = lax.all_to_all(grad_cw.reshape(16, 64, 512), "batch", 0, 0)
    with jax.named_scope("grad_normed"):
        dn_got[2] = shift_x(last_in[0], 2)
    with jax.named_scope("vectors"):
        small = sum_over((shift_x,), last_in[2])
        small = small + swap_core(small)
    cw_sent, dn_got, small = lax.optimization_barrier((cw_sent, dn_got, small))
    with jax.named_scope("conv_grads"):
        sum_cw = jnp.sum(cw_sent.astype(f32), 0)
    result = resid + blocks[0][2].astype(f32) + out_swap[0].astype(f32)
    for d in (1, 3, 2):
        result = result + out_got[d].astype(f32)
    output = result.astype(bf16).reshape(2, 128, width)
    (grad_tokens,) = call(
        k_fin, [((rows, width), bf16)],
        part_of[(0, 0)], dn_swap[0], dn_got[1], dn_got[3], dn_got[2], x, gres, gain_one,
        name="fin",
    )
    return (
        output,
        grad_tokens.reshape(2, 128, width),
        sum_cw[:, : 3 * part].reshape(64, 3, part),
        sum_cw[:, 3 * part :].T,
        small[:3],
        small[3],
        small[4],
        sum_ffn[0],
        sum_ffn[1],
        sum_ffn[2].T,
    )


def solution(mesh):
    whole = P("batch", "seq", None)
    placed = (
        whole, P("batch", None, "seq"), P("seq", "batch"), P(), P(), P(),
        P("batch", "seq"), P("batch", "seq"), P("seq", "batch"), whole,
    )
    return jax.shard_map(
        shards,
        mesh=mesh,
        in_specs=placed,
        out_specs=(
            whole, whole, P("batch", None, "seq"), P("seq", "batch"), P(), P(), P(),
            P("batch", "seq"), P("batch", "seq"), P("seq", "batch"),
        ),
        check_vma=False,
    )
```

```python
import jax
import jax.numpy as jnp
from jax import lax
from jax.experimental import pallas as pl
from jax.experimental.pallas import tpu as pltpu
from jax.sharding import PartitionSpec as P

eps = 1e-05
f32 = jnp.float32
bf16 = jnp.bfloat16
width = 1024
rows = 256
part = 128
hid = 576
MIB = 1 << 20


def swap_core(v):
    return lax.ppermute(v, "seq", [(i, i ^ 1) for i in range(8)])


def shift_x(v, d):
    return lax.ppermute(
        v, "seq", [(2 * x + c, 2 * ((x + d) % 4) + c) for x in range(4) for c in range(2)]
    )


def shift_y(v, d):
    return lax.ppermute(
        v, "batch", [(4 * z + y, 4 * z + (y + d) % 4) for z in range(4) for y in range(4)]
    )


def shift_z(v, d):
    return lax.ppermute(
        v, "batch", [(4 * z + y, 4 * ((z + d) % 4) + y) for z in range(4) for y in range(4)]
    )


def sum_over(shifts, v):
    for shift in shifts:
        v = v + shift(v, 1) + shift(v, 2) + shift(v, 3)
    return v


def after(values, *others):
    return lax.optimization_barrier((values, others))[0]


def dot(left, right, dims):
    return lax.dot_general(left, right, (dims, ((), ())), preferred_element_type=f32)


nn = ((1,), (0,))
nt = ((1,), (1,))
tn = ((0,), (0,))


def call(kernel, outs, *args, scratch=(), limit=56, smem=0, name=None):
    specs = [pl.BlockSpec(memory_space=pltpu.SMEM)] * smem + [
        pl.BlockSpec(memory_space=pltpu.VMEM)
    ] * (len(args) - smem)
    shapes = [jax.ShapeDtypeStruct(s, t) for s, t in outs]
    moved = sum(a.size * a.dtype.itemsize for a in args) + sum(
        s.size * s.dtype.itemsize for s in shapes
    )
    return pl.pallas_call(
        kernel,
        out_shape=shapes,
        in_specs=specs,
        out_specs=[pl.BlockSpec(memory_space=pltpu.VMEM)] * len(outs),
        scratch_shapes=list(scratch),
        compiler_params=pltpu.CompilerParams(vmem_limit_bytes=limit * MIB),
        cost_estimate=pl.CostEstimate(flops=1, bytes_accessed=1, transcendentals=0),
        name=name,
    )(*args)


ORDER = [(d, o) for d in (0, 1, 3, 2) for o in (0, 1)]


def k_norm(x_ref, gain_ref, out_ref):
    x = x_ref[...].astype(f32)
    scale = lax.rsqrt(jnp.mean(x * x, -1, keepdims=True) + eps)
    out_ref[...] = (x * scale * gain_ref[...].astype(f32)).astype(bf16)


def k_conv(where_ref, *refs):
    blocks = refs[:8]
    cw_ref, taps_ref, gated_ref, proj_ref, seq_ref = refs[8:]
    win = cw_ref[:, :, : 3 * part].reshape(width, 3 * part)
    seq_ref[:, :8, :] = jnp.zeros((2, 8, part), f32)
    for j in range(8):
        place = where_ref[j]
        proj = dot(blocks[j][...], win, nn)
        proj_ref[place] = proj
        bx = (proj[:, :part] * proj[:, 2 * part :]).astype(bf16).astype(f32)
        start = pl.multiple_of(8 + 128 * place, 8)
        seq_ref[:, pl.ds(start, 128), :] = bx.reshape(2, 128, part)
    taps = taps_ref[...].astype(f32)
    for i in range(8):
        for s in range(2):
            lo = 128 * i
            conv = (
                taps[0:1] * seq_ref[s, lo + 6 : lo + 134, :]
                + taps[1:2] * seq_ref[s, lo + 7 : lo + 135, :]
                + taps[2:3] * seq_ref[s, lo + 8 : lo + 136, :]
            )
            here = slice(128 * s, 128 * s + 128)
            gated_ref[i, here, :] = (proj_ref[i, here, part : 2 * part] * conv).astype(bf16)


def k_resid(where_ref, gated_ref, mine_ref, other_ref, x_ref, gain_ref, resid_ref, out_ref):
    total = x_ref[...].astype(f32)
    for j, (d, o) in enumerate(ORDER):
        weight = (mine_ref, other_ref)[o][j // 2]
        total = total + dot(gated_ref[where_ref[j]], weight, nt)
    resid_ref[...] = total
    scale = lax.rsqrt(jnp.mean(total * total, -1, keepdims=True) + eps)
    out_ref[...] = (total * scale * gain_ref[...].astype(f32)).astype(bf16)


def k_ffn(nm, no, ym, yo, w_ref, pm, po, om, oo, h_ref, g_ref):
    wg = w_ref[:, 0].reshape(width, hid)
    wu = w_ref[:, 1].reshape(width, hid)
    wd = w_ref[:, 2].reshape(width, hid)
    for o, (n, y, p, q) in enumerate(((nm, ym, pm, om), (no, yo, po, oo))):
        here = slice(rows * o, rows * o + rows)
        gate = dot(n[...], wg, nn)
        up = dot(n[...], wu, nn)
        back = dot(y[...], wd, nn)
        sigma = jax.nn.sigmoid(gate)
        silu = gate * sigma
        h = (silu * up).astype(bf16)
        gg = (back * up * sigma * (1.0 + gate * (1.0 - sigma))).astype(bf16)
        gu = (back * silu).astype(bf16)
        h_ref[here] = h
        g_ref[0, here] = gg
        g_ref[1, here] = gu
        p[...] = (dot(gg, wg, nt) + dot(gu, wu, nt)).astype(bf16)
        q[...] = dot(h, wd, nt).astype(bf16)


def k_ffn_grad(*refs):
    ns, ys = refs[:8], refs[8:16]
    hs, gs = refs[16:20], refs[20:24]
    out_ref = refs[24]
    tile = ns[0].shape[1]
    for k in range(3):
        total = jnp.zeros((tile, hid), f32)
        for j in range(8):
            here = slice(rows * (j % 2), rows * (j % 2) + rows)
            if k < 2:
                total += dot(ns[j][...], gs[j // 2][k, here], tn)
            else:
                total += dot(ys[j][...], hs[j // 2][here], tn)
        out_ref[:, k] = total.astype(bf16).reshape(tile // 64, 64, hid)


def ffn_grad(ns, ys, hs, gs):
    tile = 256
    col = pl.BlockSpec((rows, tile), lambda t: (0, t))
    h_spec = pl.BlockSpec((2 * rows, hid), lambda t: (0, 0))
    g_spec = pl.BlockSpec((2, 2 * rows, hid), lambda t: (0, 0, 0))
    return pl.pallas_call(
        k_ffn_grad,
        grid=(width // tile,),
        out_shape=jax.ShapeDtypeStruct((16, 3, 64, hid), bf16),
        in_specs=[col] * 16
        + [h_spec] * 4
        + [g_spec] * 4,
        out_specs=pl.BlockSpec((tile // 64, 3, 64, hid), lambda t: (t, 0, 0, 0)),
        compiler_params=pltpu.CompilerParams(vmem_limit_bytes=56 * MIB),
        cost_estimate=pl.CostEstimate(flops=1, bytes_accessed=1, transcendentals=0),
        name="ffn_grad",
    )(*ns, *ys, *hs, *gs)


def k_mid(where_ref, pm, sw, r1, r3, r2, resid_ref, y_ref, gain_ref, mine_ref, other_ref,
          gres_ref, low_ref, gg_ref, ggain_ref):
    total = pm[...].astype(f32) + sw[...].astype(f32)
    for r in (r1, r3, r2):
        total = total + r[...].astype(f32)
    resid = resid_ref[...]
    scale = lax.rsqrt(jnp.mean(resid * resid, -1, keepdims=True) + eps)
    unit = resid * scale
    ggain_ref[...] = jnp.sum(total * unit, 0, keepdims=True)
    scaled = total * gain_ref[...].astype(f32)
    inner = jnp.mean(scaled * resid, -1, keepdims=True)
    grad = y_ref[...].astype(f32) + scale * (scaled - unit * scale * inner)
    gres_ref[...] = grad
    low = grad.astype(bf16)
    low_ref[...] = low
    for j, (d, o) in enumerate(ORDER):
        weight = (mine_ref, other_ref)[o][j // 2]
        gg_ref[where_ref[j]] = dot(low, weight, nn).astype(bf16)


def k_wout(where_ref, low_ref, gated_ref, keep_ref, send_ref):
    low = low_ref[...]
    for j, (d, o) in enumerate(ORDER):
        out = (keep_ref, send_ref)[o]
        out[j // 2] = dot(low, gated_ref[where_ref[j]], tn).astype(bf16)


def k_conv_back(where_ref, dg_ref, proj_ref, cw_ref, taps_ref, *refs):
    outs = refs[:8]
    dp_ref, gtaps_ref, seq_ref, back_ref, abs_ref = refs[8:]
    win = cw_ref[:, :, : 3 * part].reshape(width, 3 * part)
    taps = taps_ref[...].astype(f32)
    seq_ref[:, :8, :] = jnp.zeros((2, 8, part), f32)
    back_ref[:, 1024:, :] = jnp.zeros((2, 8, part), f32)
    for i in range(8):
        for s in range(2):
            here = slice(128 * s, 128 * s + 128)
            lo = 128 * i
            b = proj_ref[i, here, :part]
            x = proj_ref[i, here, 2 * part :]
            seq_ref[s, lo + 8 : lo + 136, :] = (b * x).astype(bf16).astype(f32)
            c = proj_ref[i, here, part : 2 * part]
            back_ref[s, lo : lo + 128, :] = dg_ref[i, here, :].astype(f32) * c
    sums = [jnp.zeros((1, part), f32) for _ in range(3)]
    for i in range(8):
        for s in range(2):
            here = slice(128 * s, 128 * s + 128)
            lo = 128 * i
            back = back_ref[s, lo : lo + 128, :]
            shifted = [seq_ref[s, lo + 6 + k : lo + 134 + k, :] for k in range(3)]
            conv = taps[0:1] * shifted[0] + taps[1:2] * shifted[1] + taps[2:3] * shifted[2]
            for k in range(3):
                sums[k] = sums[k] + jnp.sum(back * shifted[k], 0, keepdims=True)
            dbx = (
                taps[0:1] * back_ref[s, lo + 2 : lo + 130, :]
                + taps[1:2] * back_ref[s, lo + 1 : lo + 129, :]
                + taps[2:3] * back
            )
            dbx = dbx.astype(bf16).astype(f32)
            abs_ref[i, here, :part] = (dbx * proj_ref[i, here, 2 * part :]).astype(bf16)
            abs_ref[i, here, part : 2 * part] = (
                dg_ref[i, here, :].astype(f32) * conv
            ).astype(bf16)
            abs_ref[i, here, 2 * part :] = (dbx * proj_ref[i, here, :part]).astype(bf16)
    gtaps_ref[...] = jnp.concatenate(sums + [jnp.zeros((5, part), f32)], 0)
    for j in range(8):
        piece = abs_ref[where_ref[j]]
        dp_ref[j] = piece
        outs[j][...] = dot(piece, win, nt).astype(bf16)


def k_win(where_ref, *refs):
    blocks = refs[:8]
    dp_ref, cw_ref, gtaps_ref, gain_ref, ggain_ref, out_ref, small_ref = refs[8:]
    total = jnp.zeros((width, 3 * part), f32)
    for j in range(8):
        total += dot(blocks[j][...], dp_ref[j], tn)
    out_ref[...] = total.astype(bf16)
    win = cw_ref[:, :, : 3 * part].reshape(width, 3 * part)
    each = jnp.sum(total * win.astype(f32), 1, keepdims=True)
    line = jnp.transpose(jnp.broadcast_to(each, (width, part)))[:1]
    small_ref[...] = jnp.concatenate(
        [
            jnp.zeros((3, width), f32),
            line / gain_ref[...].astype(f32),
            ggain_ref[...],
            jnp.zeros((3, width), f32),
        ],
        0,
    )
    here = pl.ds(pl.multiple_of(where_ref[0] * part, part), part)
    small_ref[:3, here] = gtaps_ref[:3]


def k_fin(pm, sw, r1, r3, r2, x_ref, gres_ref, gain_ref, out_ref):
    total = pm[...].astype(f32) + sw[...].astype(f32)
    for r in (r1, r3, r2):
        total = total + r[...].astype(f32)
    x = x_ref[...].astype(f32)
    scale = lax.rsqrt(jnp.mean(x * x, -1, keepdims=True) + eps)
    scaled = total * gain_ref[...].astype(f32)
    inner = jnp.mean(scaled * x, -1, keepdims=True)
    out_ref[...] = (
        gres_ref[...] + scale * (scaled - x * scale * scale * inner)
    ).astype(bf16)


def pair_sum(mine, other):
    return (mine.astype(f32) + other.astype(f32)).astype(bf16)


def shards(tokens, w_in, w_out, conv_weight, gain_norm, gain_ffn, w_gate, w_up, w_down, cotangent):
    place = lax.axis_index("seq")
    core = place % 2
    chip = place // 2
    where = jnp.stack(
        [2 * ((chip - d + 4) % 4) + (core if o == 0 else 1 - core) for d, o in ORDER]
    ).astype(jnp.int32)
    taps = lax.dynamic_slice(conv_weight, (0, place * part), (3, part))
    gain_one = gain_norm.reshape(1, width)
    gain_two = gain_ffn.reshape(1, width)
    x = tokens.reshape(rows, width)
    dy = cotangent.reshape(rows, width)

    ffn_local = jnp.stack([w_gate, w_up, w_down.T], 0)
    ffn_w = lax.all_gather(ffn_local, "batch", axis=0, tiled=False)
    (normed,) = call(k_norm, [((rows, width), bf16)], x, gain_one, name="norm")
    with jax.named_scope("normed"):
        got = {d: shift_x(normed, d) for d in (1, 3, 2)}
        got[0] = normed
        swapped = {d: swap_core(got[d]) for d in (0, 1, 3, 2)}
        normed_list = [(got, swapped)[o][d] for d, o in ORDER]
    with jax.named_scope("conv_weights"):
        conv_local = jnp.concatenate([w_in.reshape(64, 3 * part), w_out.T], 1)
        conv_w = lax.all_to_all(jnp.broadcast_to(conv_local[None], (16, 64, 512)), "batch", 0, 0)

    gated, proj = call(
        k_conv, [((8, rows, part), bf16), ((8, rows, 3 * part), f32)],
        where, *normed_list, conv_w, taps, smem=1,
        scratch=[pltpu.VMEM((2, 1032, part), f32)], name="conv",
    )
    with jax.named_scope("cotangent"):
        dy_late = after(dy, got[1], got[3], got[2])
        dy_got = {d: shift_x(dy_late, d) for d in (1, 3)}
        dy_got[0] = dy
        gated, proj, dy_got = lax.optimization_barrier((gated, proj, dy_got))
        dy_far = shift_x(after(dy, dy_got[1], dy_got[3], proj), 2)
    with jax.named_scope("gated"):
        gated_tok = lax.all_to_all(gated, "seq", 0, 0)
    with jax.named_scope("w_out"):
        wout_own = after(conv_w[:, :, 3 * part :].reshape(width, part), proj)
        wout_got = tuple(shift_x(wout_own, d) for d in (1, 3, 2))
        gated_tok, wout_got, dy_got[2] = lax.optimization_barrier((gated_tok, wout_got, dy_far))
        wout_mine = jnp.stack((wout_own,) + wout_got, 0)
        wout_other = swap_core(wout_mine)
    resid, nffn = call(
        k_resid, [((rows, width), f32), ((rows, width), bf16)],
        where, gated_tok, wout_mine, wout_other, x, gain_two, smem=1, name="resid",
    )

    with jax.named_scope("normed_ffn"):
        nffn_got = {d: shift_x(nffn, d) for d in (1, 3, 2)}
        nffn_got[0] = nffn
        nffn_swapped = {0: swap_core(nffn)}
    blocks, back_swap, out_swap, back_low, out_low = {}, {}, {}, {}, {}
    with jax.named_scope("cotangent"):
        dy_swapped = {d: swap_core(dy_got[d]) for d in (0, 1, 3, 2)}
    dy_list = [(dy_got, dy_swapped)[o][d] for d, o in ORDER]

    def ffn(d):
        return call(
            k_ffn,
            [((rows, width), bf16)] * 4 + [((2 * rows, hid), bf16), ((2, 2 * rows, hid), bf16)],
            nffn_got[d], nffn_swapped[d], dy_got[d], dy_swapped[d], ffn_w, name="ffn",
        )

    blocks[0] = ffn(0)
    with jax.named_scope("normed_ffn"):
        arrived, blocks[0] = lax.optimization_barrier(
            (tuple(nffn_got[d] for d in (1, 3, 2)), tuple(blocks[0]))
        )
        for d, piece in zip((1, 3, 2), arrived):
            nffn_got[d] = piece
            nffn_swapped[d] = swap_core(piece)
    nffn_list = [(nffn_got, nffn_swapped)[o][d] for d, o in ORDER]
    for d in (0, 1, 3, 2):
        if d:
            blocks[d] = ffn(d)
        with jax.named_scope("grad_normed_ffn"):
            back_swap[d] = swap_core(blocks[d][1])
            if d:
                back_low[d] = pair_sum(blocks[d][0], back_swap[d])
        with jax.named_scope("output"):
            out_swap[d] = swap_core(blocks[d][3])
            if d:
                out_low[d] = pair_sum(blocks[d][2], out_swap[d])
    grad_in = (
        nffn_list, dy_list, [blocks[d][4] for d in (0, 1, 3, 2)],
        [blocks[d][5] for d in (0, 1, 3, 2)],
    )
    with jax.named_scope("grad_normed_ffn"):
        grad_in = after(grad_in, back_low, out_low)
        back_got = {d: shift_x(back_low[d], (4 - d) % 4) for d in (1, 3, 2)}
    ffn_g = ffn_grad(*grad_in)
    with jax.named_scope("output"):
        out_ready = after(out_low, ffn_g, *back_got.values())
        out_got = {d: shift_x(out_ready[d], (4 - d) % 4) for d in (1, 3)}
    gres, low, dgated, ggain_two = call(
        k_mid,
        [((rows, width), f32), ((rows, width), bf16), ((8, rows, part), bf16), ((1, width), f32)],
        where, after(blocks[0][0], ffn_g), back_swap[0], back_got[1],
        back_got[3], back_got[2], resid, dy, gain_two, wout_mine, wout_other, smem=1,
        name="mid",
    )
    with jax.named_scope("ffn_grads"):
        ffn_sent = lax.psum_scatter(after(ffn_g, low), "batch", scatter_dimension=0, tiled=False)
    wout_keep, wout_send = call(
        k_wout, [((4, width, part), bf16)] * 2, where, low, gated_tok, smem=1, name="wout",
    )
    with jax.named_scope("grad_gated"):
        dgated_all = lax.all_to_all(dgated, "seq", 0, 0)
    with jax.named_scope("grad_w_out"):
        wout_both = wout_keep.astype(f32) + swap_core(wout_send).astype(f32)
        wout_low = wout_both.astype(bf16)
    with jax.named_scope("grad_w_out"):
        grad_wout = wout_both[0]
    dgated_all, out_got, wout_low, out_low = lax.optimization_barrier(
        (dgated_all, out_got, wout_low, out_low)
    )
    with jax.named_scope("output"):
        out_got[2] = shift_x(out_low[2], 2)
    with jax.named_scope("grad_w_out"):
        wout_back = [shift_x(wout_low[j], (4 - d) % 4) for j, d in ((1, 1), (2, 3), (3, 2))]
        for piece in wout_back:
            grad_wout = grad_wout + piece.astype(f32)

    conv_back = call(
        k_conv_back,
        [((rows, width), bf16)] * 8 + [((8, rows, 3 * part), bf16), ((8, part), f32)],
        where, dgated_all, proj, conv_w, taps, smem=1,
        scratch=[
            pltpu.VMEM((2, 1032, part), f32),
            pltpu.VMEM((2, 1032, part), f32),
            pltpu.VMEM((8, rows, 3 * part), bf16),
        ],
        name="conv_back",
    )
    part_of = {(d, o): conv_back[j] for j, (d, o) in enumerate(ORDER)}
    dproj, gtaps = conv_back[8:]
    with jax.named_scope("grad_normed"):
        dn_swap = {d: swap_core(part_of[(d, 1)]) for d in (1, 3, 2, 0)}
    grad_win, small = call(
        k_win, [((width, 3 * part), bf16), ((8, width), f32)],
        where, *normed_list, dproj, conv_w, gtaps, gain_one, ggain_two, smem=1, name="win",
    )
    with jax.named_scope("grad_normed"):
        dn_keep = {d: part_of[(d, 0)] for d in (1, 3, 2)}
        dn_keep, out_got = lax.optimization_barrier((after(dn_keep, grad_win), out_got))
        dn_low = {d: pair_sum(dn_keep[d], dn_swap[d]) for d in (1, 3, 2)}
        dn_got = {d: shift_x(dn_low[d], (4 - d) % 4) for d in (1, 3)}
    with jax.named_scope("vectors"):
        small = after(small, *dn_low.values())
        small = sum_over((shift_z, shift_y), small)
    grad_cw = jnp.concatenate([grad_win, grad_wout.astype(bf16)], 1)
    with jax.named_scope("grad_normed"):
        dn_got[2] = shift_x(dn_low[2], 2)
    grad_cw, small, dn_got, sum_ffn = lax.optimization_barrier(
        (grad_cw, small, dn_got, ffn_sent.astype(f32))
    )
    with jax.named_scope("conv_grads"):
        cw_sent = lax.all_to_all(grad_cw.reshape(16, 64, 512), "batch", 0, 0)
    with jax.named_scope("vectors"):
        small = sum_over((shift_x,), small)
        cw_sent, small = lax.optimization_barrier((cw_sent, small))
        small = small + swap_core(small)
    with jax.named_scope("conv_grads"):
        sum_cw = jnp.sum(cw_sent.astype(f32), 0)
    result = resid + blocks[0][2].astype(f32) + out_swap[0].astype(f32)
    for d in (1, 3, 2):
        result = result + out_got[d].astype(f32)
    output = result.astype(bf16).reshape(2, 128, width)
    (grad_tokens,) = call(
        k_fin, [((rows, width), bf16)],
        part_of[(0, 0)], dn_swap[0], dn_got[1], dn_got[3], dn_got[2], x, gres, gain_one,
        name="fin",
    )
    return (
        output,
        grad_tokens.reshape(2, 128, width),
        sum_cw[:, : 3 * part].reshape(64, 3, part),
        sum_cw[:, 3 * part :].T,
        small[:3],
        small[3],
        small[4],
        sum_ffn[0],
        sum_ffn[1],
        sum_ffn[2].T,
    )


def solution(mesh):
    whole = P("batch", "seq", None)
    placed = (
        whole, P("batch", None, "seq"), P("seq", "batch"), P(), P(), P(),
        P("batch", "seq"), P("batch", "seq"), P("seq", "batch"), whole,
    )
    return jax.shard_map(
        shards,
        mesh=mesh,
        in_specs=placed,
        out_specs=(
            whole, whole, P("batch", None, "seq"), P("seq", "batch"), P(), P(), P(),
            P("batch", "seq"), P("batch", "seq"), P("seq", "batch"),
        ),
        check_vma=False,
    )
```

```python
import jax
import jax.numpy as jnp
from jax import lax
from jax.experimental import pallas as pl
from jax.experimental.pallas import tpu as pltpu
from jax.sharding import PartitionSpec as P

eps = 1e-05
f32 = jnp.float32
bf16 = jnp.bfloat16
width = 1024
rows = 256
part = 128
hid = 576
MIB = 1 << 20


def swap_core(v):
    return lax.ppermute(v, "seq", [(i, i ^ 1) for i in range(8)])


def shift_x(v, d):
    return lax.ppermute(
        v, "seq", [(2 * x + c, 2 * ((x + d) % 4) + c) for x in range(4) for c in range(2)]
    )


def shift_y(v, d):
    return lax.ppermute(
        v, "batch", [(4 * z + y, 4 * z + (y + d) % 4) for z in range(4) for y in range(4)]
    )


def shift_z(v, d):
    return lax.ppermute(
        v, "batch", [(4 * z + y, 4 * ((z + d) % 4) + y) for z in range(4) for y in range(4)]
    )


def sum_over(shifts, v):
    for shift in shifts:
        v = v + shift(v, 1) + shift(v, 2) + shift(v, 3)
    return v


def after(values, *others):
    return lax.optimization_barrier((values, others))[0]


def dot(left, right, dims):
    return lax.dot_general(left, right, (dims, ((), ())), preferred_element_type=f32)


nn = ((1,), (0,))
nt = ((1,), (1,))
tn = ((0,), (0,))


def call(kernel, outs, *args, scratch=(), limit=56, smem=0, name=None):
    specs = [pl.BlockSpec(memory_space=pltpu.SMEM)] * smem + [
        pl.BlockSpec(memory_space=pltpu.VMEM)
    ] * (len(args) - smem)
    shapes = [jax.ShapeDtypeStruct(s, t) for s, t in outs]
    moved = sum(a.size * a.dtype.itemsize for a in args) + sum(
        s.size * s.dtype.itemsize for s in shapes
    )
    return pl.pallas_call(
        kernel,
        out_shape=shapes,
        in_specs=specs,
        out_specs=[pl.BlockSpec(memory_space=pltpu.VMEM)] * len(outs),
        scratch_shapes=list(scratch),
        compiler_params=pltpu.CompilerParams(vmem_limit_bytes=limit * MIB),
        cost_estimate=pl.CostEstimate(flops=1, bytes_accessed=1, transcendentals=0),
        name=name,
    )(*args)


ORDER = [(d, o) for d in (0, 1, 3, 2) for o in (0, 1)]


def k_norm(x_ref, gain_ref, out_ref):
    x = x_ref[...].astype(f32)
    scale = lax.rsqrt(jnp.mean(x * x, -1, keepdims=True) + eps)
    out_ref[...] = (x * scale * gain_ref[...].astype(f32)).astype(bf16)


def k_conv(where_ref, *refs):
    blocks = refs[:8]
    cw_ref, taps_ref, gated_ref, proj_ref, seq_ref = refs[8:]
    win = cw_ref[:, :, : 3 * part].reshape(width, 3 * part)
    seq_ref[:, :8, :] = jnp.zeros((2, 8, part), f32)
    for j in range(8):
        place = where_ref[j]
        proj = dot(blocks[j][...], win, nn)
        proj_ref[place] = proj
        bx = (proj[:, :part] * proj[:, 2 * part :]).astype(bf16).astype(f32)
        start = pl.multiple_of(8 + 128 * place, 8)
        seq_ref[:, pl.ds(start, 128), :] = bx.reshape(2, 128, part)
    taps = taps_ref[...].astype(f32)
    for i in range(8):
        for s in range(2):
            lo = 128 * i
            conv = (
                taps[0:1] * seq_ref[s, lo + 6 : lo + 134, :]
                + taps[1:2] * seq_ref[s, lo + 7 : lo + 135, :]
                + taps[2:3] * seq_ref[s, lo + 8 : lo + 136, :]
            )
            here = slice(128 * s, 128 * s + 128)
            gated_ref[i, here, :] = (proj_ref[i, here, part : 2 * part] * conv).astype(bf16)


def k_resid(where_ref, gated_ref, mine_ref, other_ref, x_ref, gain_ref, resid_ref, out_ref):
    total = x_ref[...].astype(f32)
    for j, (d, o) in enumerate(ORDER):
        weight = (mine_ref, other_ref)[o][j // 2]
        total = total + dot(gated_ref[where_ref[j]], weight, nt)
    resid_ref[...] = total
    scale = lax.rsqrt(jnp.mean(total * total, -1, keepdims=True) + eps)
    out_ref[...] = (total * scale * gain_ref[...].astype(f32)).astype(bf16)


def k_ffn(nm, no, ym, yo, w_ref, pm, po, om, oo, h_ref, g_ref):
    wg = w_ref[:, 0].reshape(width, hid)
    wu = w_ref[:, 1].reshape(width, hid)
    wd = w_ref[:, 2].reshape(width, hid)
    for o, (n, y, p, q) in enumerate(((nm, ym, pm, om), (no, yo, po, oo))):
        here = slice(rows * o, rows * o + rows)
        gate = dot(n[...], wg, nn)
        up = dot(n[...], wu, nn)
        back = dot(y[...], wd, nn)
        sigma = jax.nn.sigmoid(gate)
        silu = gate * sigma
        h = (silu * up).astype(bf16)
        gg = (back * up * sigma * (1.0 + gate * (1.0 - sigma))).astype(bf16)
        gu = (back * silu).astype(bf16)
        h_ref[here] = h
        g_ref[0, here] = gg
        g_ref[1, here] = gu
        p[...] = (dot(gg, wg, nt) + dot(gu, wu, nt)).astype(bf16)
        q[...] = dot(h, wd, nt).astype(bf16)


def k_ffn_grad(*refs):
    ns, ys = refs[:8], refs[8:16]
    hs, gs = refs[16:20], refs[20:24]
    out_ref = refs[24]
    tile = ns[0].shape[1]
    for k in range(3):
        total = jnp.zeros((tile, hid), f32)
        for j in range(8):
            here = slice(rows * (j % 2), rows * (j % 2) + rows)
            if k < 2:
                total += dot(ns[j][...], gs[j // 2][k, here], tn)
            else:
                total += dot(ys[j][...], hs[j // 2][here], tn)
        out_ref[:, k] = total.astype(bf16).reshape(tile // 64, 64, hid)


def ffn_grad(ns, ys, hs, gs):
    tile = 256
    col = pl.BlockSpec((rows, tile), lambda t: (0, t))
    h_spec = pl.BlockSpec((2 * rows, hid), lambda t: (0, 0))
    g_spec = pl.BlockSpec((2, 2 * rows, hid), lambda t: (0, 0, 0))
    return pl.pallas_call(
        k_ffn_grad,
        grid=(width // tile,),
        out_shape=jax.ShapeDtypeStruct((16, 3, 64, hid), bf16),
        in_specs=[col] * 16
        + [h_spec] * 4
        + [g_spec] * 4,
        out_specs=pl.BlockSpec((tile // 64, 3, 64, hid), lambda t: (t, 0, 0, 0)),
        compiler_params=pltpu.CompilerParams(vmem_limit_bytes=56 * MIB),
        cost_estimate=pl.CostEstimate(flops=1, bytes_accessed=1, transcendentals=0),
        name="ffn_grad",
    )(*ns, *ys, *hs, *gs)


def k_mid(where_ref, pm, sw, r1, r3, r2, resid_ref, y_ref, gain_ref, mine_ref, other_ref,
          gres_ref, low_ref, gg_ref, ggain_ref):
    total = pm[...].astype(f32) + sw[...].astype(f32)
    for r in (r1, r3, r2):
        total = total + r[...].astype(f32)
    resid = resid_ref[...]
    scale = lax.rsqrt(jnp.mean(resid * resid, -1, keepdims=True) + eps)
    unit = resid * scale
    ggain_ref[...] = jnp.sum(total * unit, 0, keepdims=True)
    scaled = total * gain_ref[...].astype(f32)
    inner = jnp.mean(scaled * resid, -1, keepdims=True)
    grad = y_ref[...].astype(f32) + scale * (scaled - unit * scale * inner)
    gres_ref[...] = grad
    low = grad.astype(bf16)
    low_ref[...] = low
    for j, (d, o) in enumerate(ORDER):
        weight = (mine_ref, other_ref)[o][j // 2]
        gg_ref[where_ref[j]] = dot(low, weight, nn).astype(bf16)


def k_wout(where_ref, low_ref, gated_ref, keep_ref, send_ref):
    low = low_ref[...]
    for j, (d, o) in enumerate(ORDER):
        out = (keep_ref, send_ref)[o]
        out[j // 2] = dot(low, gated_ref[where_ref[j]], tn).astype(bf16)


def k_conv_back(where_ref, dg_ref, proj_ref, cw_ref, taps_ref, *refs):
    outs = refs[:8]
    dp_ref, gtaps_ref, seq_ref, back_ref, abs_ref = refs[8:]
    win = cw_ref[:, :, : 3 * part].reshape(width, 3 * part)
    taps = taps_ref[...].astype(f32)
    seq_ref[:, :8, :] = jnp.zeros((2, 8, part), f32)
    back_ref[:, 1024:, :] = jnp.zeros((2, 8, part), f32)
    for i in range(8):
        for s in range(2):
            here = slice(128 * s, 128 * s + 128)
            lo = 128 * i
            b = proj_ref[i, here, :part]
            x = proj_ref[i, here, 2 * part :]
            seq_ref[s, lo + 8 : lo + 136, :] = (b * x).astype(bf16).astype(f32)
            c = proj_ref[i, here, part : 2 * part]
            back_ref[s, lo : lo + 128, :] = dg_ref[i, here, :].astype(f32) * c
    sums = [jnp.zeros((1, part), f32) for _ in range(3)]
    for i in range(8):
        for s in range(2):
            here = slice(128 * s, 128 * s + 128)
            lo = 128 * i
            back = back_ref[s, lo : lo + 128, :]
            shifted = [seq_ref[s, lo + 6 + k : lo + 134 + k, :] for k in range(3)]
            conv = taps[0:1] * shifted[0] + taps[1:2] * shifted[1] + taps[2:3] * shifted[2]
            for k in range(3):
                sums[k] = sums[k] + jnp.sum(back * shifted[k], 0, keepdims=True)
            dbx = (
                taps[0:1] * back_ref[s, lo + 2 : lo + 130, :]
                + taps[1:2] * back_ref[s, lo + 1 : lo + 129, :]
                + taps[2:3] * back
            )
            dbx = dbx.astype(bf16).astype(f32)
            abs_ref[i, here, :part] = (dbx * proj_ref[i, here, 2 * part :]).astype(bf16)
            abs_ref[i, here, part : 2 * part] = (
                dg_ref[i, here, :].astype(f32) * conv
            ).astype(bf16)
            abs_ref[i, here, 2 * part :] = (dbx * proj_ref[i, here, :part]).astype(bf16)
    gtaps_ref[...] = jnp.concatenate(sums + [jnp.zeros((5, part), f32)], 0)
    for j in range(8):
        piece = abs_ref[where_ref[j]]
        dp_ref[j] = piece
        outs[j][...] = dot(piece, win, nt).astype(bf16)


def k_win(where_ref, *refs):
    blocks = refs[:8]
    dp_ref, cw_ref, gtaps_ref, gain_ref, ggain_ref, out_ref, small_ref = refs[8:]
    total = jnp.zeros((width, 3 * part), f32)
    for j in range(8):
        total += dot(blocks[j][...], dp_ref[j], tn)
    out_ref[...] = total.astype(bf16)
    win = cw_ref[:, :, : 3 * part].reshape(width, 3 * part)
    each = jnp.sum(total * win.astype(f32), 1, keepdims=True)
    line = jnp.transpose(jnp.broadcast_to(each, (width, part)))[:1]
    small_ref[...] = jnp.concatenate(
        [
            jnp.zeros((3, width), f32),
            line / gain_ref[...].astype(f32),
            ggain_ref[...],
            jnp.zeros((3, width), f32),
        ],
        0,
    )
    here = pl.ds(pl.multiple_of(where_ref[0] * part, part), part)
    small_ref[:3, here] = gtaps_ref[:3]


def k_fin(pm, sw, r1, r3, r2, x_ref, gres_ref, gain_ref, out_ref):
    total = pm[...].astype(f32) + sw[...].astype(f32)
    for r in (r1, r3, r2):
        total = total + r[...].astype(f32)
    x = x_ref[...].astype(f32)
    scale = lax.rsqrt(jnp.mean(x * x, -1, keepdims=True) + eps)
    scaled = total * gain_ref[...].astype(f32)
    inner = jnp.mean(scaled * x, -1, keepdims=True)
    out_ref[...] = (
        gres_ref[...] + scale * (scaled - x * scale * scale * inner)
    ).astype(bf16)


def pair_sum(mine, other):
    return (mine.astype(f32) + other.astype(f32)).astype(bf16)


def shards(tokens, w_in, w_out, conv_weight, gain_norm, gain_ffn, w_gate, w_up, w_down, cotangent):
    place = lax.axis_index("seq")
    core = place % 2
    chip = place // 2
    where = jnp.stack(
        [2 * ((chip - d + 4) % 4) + (core if o == 0 else 1 - core) for d, o in ORDER]
    ).astype(jnp.int32)
    taps = lax.dynamic_slice(conv_weight, (0, place * part), (3, part))
    gain_one = gain_norm.reshape(1, width)
    gain_two = gain_ffn.reshape(1, width)
    x = tokens.reshape(rows, width)
    dy = cotangent.reshape(rows, width)

    ffn_local = jnp.stack([w_gate, w_up, w_down.T], 0)
    ffn_w = lax.all_gather(ffn_local, "batch", axis=0, tiled=False)
    (normed,) = call(k_norm, [((rows, width), bf16)], x, gain_one, name="norm")
    with jax.named_scope("normed"):
        got = {d: shift_x(normed, d) for d in (1, 3, 2)}
        got[0] = normed
        swapped = {d: swap_core(got[d]) for d in (0, 1, 3, 2)}
        normed_list = [(got, swapped)[o][d] for d, o in ORDER]
    with jax.named_scope("conv_weights"):
        conv_local = jnp.concatenate([w_in.reshape(64, 3 * part), w_out.T], 1)
        conv_w = lax.all_to_all(jnp.broadcast_to(conv_local[None], (16, 64, 512)), "batch", 0, 0)

    gated, proj = call(
        k_conv, [((8, rows, part), bf16), ((8, rows, 3 * part), f32)],
        where, *normed_list, conv_w, taps, smem=1,
        scratch=[pltpu.VMEM((2, 1032, part), f32)], name="conv",
    )
    with jax.named_scope("cotangent"):
        dy_late = after(dy, got[1], got[3], got[2])
        dy_got = {d: shift_x(dy_late, d) for d in (1, 3)}
        dy_got[0] = dy
        gated, proj, dy_got = lax.optimization_barrier((gated, proj, dy_got))
        dy_far = shift_x(after(dy, dy_got[1], dy_got[3], proj), 2)
    with jax.named_scope("gated"):
        gated_tok = lax.all_to_all(gated, "seq", 0, 0)
    with jax.named_scope("w_out"):
        wout_own = after(conv_w[:, :, 3 * part :].reshape(width, part), proj)
        wout_got = tuple(shift_x(wout_own, d) for d in (1, 3, 2))
        gated_tok, wout_got, dy_got[2] = lax.optimization_barrier((gated_tok, wout_got, dy_far))
        wout_mine = jnp.stack((wout_own,) + wout_got, 0)
        wout_other = swap_core(wout_mine)
    resid, nffn = call(
        k_resid, [((rows, width), f32), ((rows, width), bf16)],
        where, gated_tok, wout_mine, wout_other, x, gain_two, smem=1, name="resid",
    )

    with jax.named_scope("normed_ffn"):
        nffn_got = {d: shift_x(nffn, d) for d in (1, 3, 2)}
        nffn_got[0] = nffn
        nffn_swapped = {0: swap_core(nffn)}
    blocks, back_swap, out_swap, back_low, out_low = {}, {}, {}, {}, {}
    with jax.named_scope("cotangent"):
        dy_swapped = {d: swap_core(dy_got[d]) for d in (0, 1, 3, 2)}
    dy_list = [(dy_got, dy_swapped)[o][d] for d, o in ORDER]

    def ffn(d):
        return call(
            k_ffn,
            [((rows, width), bf16)] * 4 + [((2 * rows, hid), bf16), ((2, 2 * rows, hid), bf16)],
            nffn_got[d], nffn_swapped[d], dy_got[d], dy_swapped[d], ffn_w, limit=28, name="ffn",
        )

    blocks[0] = ffn(0)
    with jax.named_scope("normed_ffn"):
        arrived, blocks[0] = lax.optimization_barrier(
            (tuple(nffn_got[d] for d in (1, 3, 2)), tuple(blocks[0]))
        )
        for d, piece in zip((1, 3, 2), arrived):
            nffn_got[d] = piece
            nffn_swapped[d] = swap_core(piece)
    nffn_list = [(nffn_got, nffn_swapped)[o][d] for d, o in ORDER]
    for d in (0, 1, 3, 2):
        if d:
            blocks[d] = ffn(d)
        with jax.named_scope("grad_normed_ffn"):
            back_swap[d] = swap_core(blocks[d][1])
            if d:
                back_low[d] = pair_sum(blocks[d][0], back_swap[d])
        with jax.named_scope("output"):
            out_swap[d] = swap_core(blocks[d][3])
            if d:
                out_low[d] = pair_sum(blocks[d][2], out_swap[d])
    grad_in = (
        nffn_list, dy_list, [blocks[d][4] for d in (0, 1, 3, 2)],
        [blocks[d][5] for d in (0, 1, 3, 2)],
    )
    with jax.named_scope("grad_normed_ffn"):
        grad_in = after(grad_in, back_low, out_low)
        back_got = {d: shift_x(back_low[d], (4 - d) % 4) for d in (1, 3, 2)}
    ffn_g = ffn_grad(*grad_in)
    with jax.named_scope("output"):
        out_ready = after(out_low, ffn_g, *back_got.values())
        out_got = {d: shift_x(out_ready[d], (4 - d) % 4) for d in (1, 3)}
    gres, low, dgated, ggain_two = call(
        k_mid,
        [((rows, width), f32), ((rows, width), bf16), ((8, rows, part), bf16), ((1, width), f32)],
        where, after(blocks[0][0], ffn_g), back_swap[0], back_got[1],
        back_got[3], back_got[2], resid, dy, gain_two, wout_mine, wout_other, smem=1,
        name="mid",
    )
    with jax.named_scope("ffn_grads"):
        ffn_sent = lax.psum_scatter(after(ffn_g, low), "batch", scatter_dimension=0, tiled=False)
    wout_keep, wout_send = call(
        k_wout, [((4, width, part), bf16)] * 2, where, low, gated_tok, smem=1, name="wout",
    )
    with jax.named_scope("grad_gated"):
        dgated_all = lax.all_to_all(dgated, "seq", 0, 0)
    with jax.named_scope("grad_w_out"):
        wout_both = wout_keep.astype(f32) + swap_core(wout_send).astype(f32)
        wout_low = wout_both.astype(bf16)
    with jax.named_scope("grad_w_out"):
        grad_wout = wout_both[0]
    dgated_all, out_got, wout_low, out_low = lax.optimization_barrier(
        (dgated_all, out_got, wout_low, out_low)
    )
    with jax.named_scope("output"):
        out_got[2] = shift_x(out_low[2], 2)
    with jax.named_scope("grad_w_out"):
        wout_back = [shift_x(wout_low[j], (4 - d) % 4) for j, d in ((1, 1), (2, 3), (3, 2))]
        for piece in wout_back:
            grad_wout = grad_wout + piece.astype(f32)

    conv_back = call(
        k_conv_back,
        [((rows, width), bf16)] * 8 + [((8, rows, 3 * part), bf16), ((8, part), f32)],
        where, dgated_all, proj, conv_w, taps, smem=1,
        scratch=[
            pltpu.VMEM((2, 1032, part), f32),
            pltpu.VMEM((2, 1032, part), f32),
            pltpu.VMEM((8, rows, 3 * part), bf16),
        ],
        name="conv_back",
    )
    part_of = {(d, o): conv_back[j] for j, (d, o) in enumerate(ORDER)}
    dproj, gtaps = conv_back[8:]
    with jax.named_scope("grad_normed"):
        dn_swap = {d: swap_core(part_of[(d, 1)]) for d in (1, 3, 2, 0)}
    grad_win, small = call(
        k_win, [((width, 3 * part), bf16), ((8, width), f32)],
        where, *normed_list, dproj, conv_w, gtaps, gain_one, ggain_two, smem=1, name="win",
    )
    with jax.named_scope("grad_normed"):
        dn_keep = {d: part_of[(d, 0)] for d in (1, 3, 2)}
        dn_keep, out_got = lax.optimization_barrier((after(dn_keep, grad_win), out_got))
        dn_low = {d: pair_sum(dn_keep[d], dn_swap[d]) for d in (1, 3, 2)}
        dn_got = {d: shift_x(dn_low[d], (4 - d) % 4) for d in (1, 3)}
    with jax.named_scope("vectors"):
        small = after(small, *dn_low.values())
        small = sum_over((shift_z, shift_y), small)
    grad_cw = jnp.concatenate([grad_win, grad_wout.astype(bf16)], 1)
    last_in = (dn_low[2], grad_cw, small)
    last_in = after(last_in, dn_got[1], dn_got[3])
    with jax.named_scope("conv_grads"):
        grad_cw, sum_ffn = lax.optimization_barrier((last_in[1], ffn_sent.astype(f32)))
        cw_sent = lax.all_to_all(grad_cw.reshape(16, 64, 512), "batch", 0, 0)
    with jax.named_scope("grad_normed"):
        dn_got[2] = shift_x(last_in[0], 2)
    with jax.named_scope("vectors"):
        small = sum_over((shift_x,), last_in[2])
        small = small + swap_core(small)
    cw_sent, dn_got, small = lax.optimization_barrier((cw_sent, dn_got, small))
    with jax.named_scope("conv_grads"):
        sum_cw = jnp.sum(cw_sent.astype(f32), 0)
    result = resid + blocks[0][2].astype(f32) + out_swap[0].astype(f32)
    for d in (1, 3, 2):
        result = result + out_got[d].astype(f32)
    output = result.astype(bf16).reshape(2, 128, width)
    (grad_tokens,) = call(
        k_fin, [((rows, width), bf16)],
        part_of[(0, 0)], dn_swap[0], dn_got[1], dn_got[3], dn_got[2], x, gres, gain_one,
        name="fin",
    )
    return (
        output,
        grad_tokens.reshape(2, 128, width),
        sum_cw[:, : 3 * part].reshape(64, 3, part),
        sum_cw[:, 3 * part :].T,
        small[:3],
        small[3],
        small[4],
        sum_ffn[0],
        sum_ffn[1],
        sum_ffn[2].T,
    )


def solution(mesh):
    whole = P("batch", "seq", None)
    placed = (
        whole, P("batch", None, "seq"), P("seq", "batch"), P(), P(), P(),
        P("batch", "seq"), P("batch", "seq"), P("seq", "batch"), whole,
    )
    return jax.shard_map(
        shards,
        mesh=mesh,
        in_specs=placed,
        out_specs=(
            whole, whole, P("batch", None, "seq"), P("seq", "batch"), P(), P(), P(),
            P("batch", "seq"), P("batch", "seq"), P("seq", "batch"),
        ),
        check_vma=False,
    )
```
